256 devices in a mesh: dp: 16 (over x, y_hi, core), tensor: 16 (over y_lo, z).
Axes of the slice: x: 4, y: 4 (y_hi: 2, y_lo: 2; y = y_hi * 2 + y_lo), z: 8, core: 2. Of those that a mesh axis runs over, the one named last changes fastest.
Arguments:
- tokens: bfloat16 [4096, 4096], P(('dp', 'tensor')), may hold values from -6 to 6
- weight_tiles: bfloat16 [16, 128, 2, 128, 128], P('tensor', 'dp'), may hold values from -0.125 to 0.125
- keep_mask: int32 [2, 32, 112], P(None, None, 'tensor'), may hold values from 0 to 1, as said below
- cotangent: bfloat16 [4096, 14336], P('dp', 'tensor'), may hold values from -6 to 6
Outputs:
- hidden: bfloat16 [4096, 14336], P('dp', 'tensor')
- grad_tokens: bfloat16 [4096, 4096], P(('dp', 'tensor'))
- tile_grads: float32 [16, 128, 2, 128, 128], P('tensor', 'dp')
The draws below stay inside these ranges and needn't reach their ends.
Inputs may be any that keep to these rules, and one draw needn't show every extreme that they name: keep_mask[m, r, t * 7 + c] is 1 where tile (r, c) of tensor shard t's grid is kept in matrix m; each shard's grid of each matrix keeps 64 to 128 tiles, and some shard exactly 128.
All inputs are finite; a program needn't handle non-finite values.
Results may differ from the reference program's by a relative error of at most 0.0049.
Values may be sent and summed in bfloat16 or wider, within the bound.
No kernel may reach another device: no remote copies, remote signals or barrier semaphores. Data moves between devices by JAX's collectives and lax.ppermute only.
A program may use at most 128 MiB of HBM per device.

```python
import jax
import jax.numpy as jnp
from jax import lax

B = 128
D = 4096
FF = 14336
TOK_GRP = 256
DB = 32
CB = 7
CAP = 128
CMIN = 64
TOKENS = 4096
N_DP = 16
N_TENSOR = 16


def draw_keep_mask(key, part):
    shard_count = FF // (B * CB)
    grid_size = DB * CB
    count_key, fullest_key, order_key = jax.random.split(key, 3)
    counts = jax.random.randint(count_key, (2, shard_count), CMIN, CAP + 1)
    fullest = jax.random.randint(fullest_key, (2,), 0, shard_count)
    counts = jnp.where(jnp.arange(shard_count)[None, :] == fullest[:, None], CAP, counts)
    order_keys = jax.random.split(order_key, 2 * shard_count)
    rank_table = jax.vmap(lambda single_key: jax.random.permutation(single_key, grid_size))(order_keys)
    rank_table = rank_table.reshape(2, shard_count, DB, CB)
    kept_tiles = (rank_table < counts[:, :, None, None]).astype(jnp.int32)
    return kept_tiles.transpose(0, 2, 1, 3).reshape(2, DB, shard_count * CB)


def level_of(stream_key, dims, pieces, smallest, high):
    factor_of = 1.0
    for dim, shards_of in pieces:
        heights = jax.random.uniform(jax.random.fold_in(jax.random.fold_in(stream_key, 6), dim), (shards_of,), jnp.float32, smallest / len(pieces), high / len(pieces))
        factor_of = factor_of * jnp.repeat(jnp.exp(heights), dims[dim] // shards_of).reshape((-1,) + (1,) * (len(dims) - 1 - dim))
    return factor_of


def gaussian(stream_key, extent, scale, reach, pieces=(), kind=jnp.bfloat16):
    result = scale * jax.random.normal(stream_key, extent, jnp.float32)
    if pieces:
        result = result * level_of(stream_key, extent, pieces, -0.22, 0.18)
    return jnp.clip(result, -reach, reach).astype(kind)


def setup_inputs(seed: int = 0) -> dict:
    key_of = jax.random.split(jax.random.key(seed), 5)
    return {
        "tokens": gaussian(key_of[0], (TOKENS, D), 1.0, 6.0, ((0, 256),)),
        "weight_tiles": gaussian(key_of[1], (N_TENSOR, CAP, 2, B, B), (D // 2) ** -0.5, 0.125, ((0, 16), (1, 16))),
        "keep_mask": draw_keep_mask(jax.random.fold_in(key_of[4], 71), 0),
        "cotangent": gaussian(key_of[3], (TOKENS, FF), 1.0, 6.0, ((0, 16), (1, 16))),
    }


def shard_slots(keep_mask):
    matrix_count, rows_blocks, all_columns = keep_mask.shape
    shard_count = all_columns // CB
    local_keep = keep_mask.reshape(matrix_count, rows_blocks, shard_count, CB)
    local_keep = local_keep.transpose(0, 2, 1, 3).reshape(matrix_count, shard_count, rows_blocks * CB)
    slot_order = jnp.cumsum(local_keep, axis=2) - 1
    return local_keep, slot_order.astype(jnp.int32)


def dense_weight(weight_tiles, local_keep, slot_order, matrix_id):
    shard_count = local_keep.shape[1]
    chosen = jnp.clip(slot_order[matrix_id], 0, CAP - 1).astype(jnp.int32)
    picked = jax.vmap(lambda tile_list, index_list: jnp.take(tile_list, index_list, axis=0))(weight_tiles[:, :, matrix_id], chosen)
    picked = jnp.where(local_keep[matrix_id][:, :, None, None] == 1, picked, jnp.zeros((), picked.dtype))
    picked = picked.reshape(shard_count, DB, CB, B, B).transpose(1, 3, 0, 2, 4)
    return picked.reshape(D, FF)


def reference(tokens, weight_tiles, keep_mask, cotangent):
    local_keep, slot_order = shard_slots(keep_mask)
    gate_weight = dense_weight(weight_tiles, local_keep, slot_order, 0)
    up_weight = dense_weight(weight_tiles, local_keep, slot_order, 1)
    gate_sum = jnp.dot(tokens, gate_weight, preferred_element_type=jnp.float32)
    upward = jnp.dot(tokens, up_weight, preferred_element_type=jnp.float32)
    sigma = jax.nn.sigmoid(gate_sum)
    hidden = (gate_sum * sigma * upward).astype(jnp.bfloat16)
    grad_out = cotangent.astype(jnp.float32)
    grad_up = (grad_out * gate_sum * sigma).astype(jnp.bfloat16)
    grad_gate = (grad_out * upward * sigma * (1.0 + gate_sum * (1.0 - sigma))).astype(jnp.bfloat16)
    grad_tokens = (jnp.dot(grad_gate, gate_weight.T, preferred_element_type=jnp.float32)
                   + jnp.dot(grad_up, up_weight.T, preferred_element_type=jnp.float32)).astype(jnp.bfloat16)

    group_tokens = tokens.reshape(N_DP, TOK_GRP, D)
    group_gate = grad_gate.reshape(N_DP, TOK_GRP, FF)
    group_up = grad_up.reshape(N_DP, TOK_GRP, FF)

    def add_group(running, items):
        token_part, gate_part, up_part = items
        gate_term = jnp.dot(token_part.T, gate_part, preferred_element_type=jnp.float32)
        up_term = jnp.dot(token_part.T, up_part, preferred_element_type=jnp.float32)
        return running + jnp.stack([gate_term, up_term]), None

    total_sum, unused = lax.scan(add_group, jnp.zeros((2, D, FF), jnp.float32), (group_tokens, group_gate, group_up))
    total_sum = total_sum * (1.0 / N_DP)
    grid_tiles = total_sum.reshape(2, DB, B, N_TENSOR, CB, B).transpose(3, 0, 1, 4, 2, 5)
    grid_tiles = grid_tiles.reshape(N_TENSOR, 2, DB * CB, B, B)
    slot_ids = jnp.arange(CAP, dtype=jnp.int32)
    matches = jnp.logical_and(slot_order[:, :, :, None] == slot_ids[None, None, None, :],
                              local_keep[:, :, :, None] == 1).astype(jnp.int32)
    places = jnp.arange(DB * CB, dtype=jnp.int32)
    position = jnp.sum(matches * places[None, None, :, None], axis=2).transpose(1, 0, 2)
    live_slot = jnp.sum(matches, axis=2).transpose(1, 0, 2)
    taken = jax.vmap(jax.vmap(lambda tile_list, index_list: jnp.take(tile_list, index_list, axis=0)))(grid_tiles, position)
    taken = jnp.where(live_slot[:, :, :, None, None] == 1, taken, jnp.zeros((), taken.dtype))
    tile_grads = taken.transpose(0, 2, 1, 3, 4)
    return hidden, grad_tokens, tile_grads
```

```python
import functools

import jax
import jax.numpy as jnp
from jax import lax
from jax.experimental import pallas as pl
from jax.experimental.pallas import tpu as pltpu
from jax.sharding import PartitionSpec as P

TILE = 128
ROWS = 32
COLS = 7
CAP = 128
PER = 8
GROUP = 256
WIDTH = ROWS * TILE
HIDE = COLS * TILE
DEAD = ROWS * COLS
XS, YS, CS = 4, 2, 2
ZS, YL = 8, 2


def dp_perm(move):
    def index(x, y, c):
        return (x * YS + y) * CS + c

    return [
        (index(x, y, c), index(*move(x, y, c)))
        for x in range(XS)
        for y in range(YS)
        for c in range(CS)
    ]


X_UP = dp_perm(lambda x, y, c: ((x + 1) % XS, y, c))
X_DOWN = dp_perm(lambda x, y, c: ((x - 1) % XS, y, c))
Y_SWAP = dp_perm(lambda x, y, c: (x, 1 - y, c))
C_SWAP = dp_perm(lambda x, y, c: (x, y, 1 - c))
L_SWAP = [(l * ZS + z, (1 - l) * ZS + z) for l in range(YL) for z in range(ZS)]
Z_RINGS = [[l * ZS + z for z in range(ZS)] for l in range(YL)]

BLOCKS = {(1, 1): 0, (3, 1): 1, (2, 1): 2, (0, 1): 3, (2, 0): 4, (1, 0): 5, (3, 0): 6, (0, 0): 7}


def kernel(
    place, target, ranks,
    piece_a, piece_b, piece_c, piece_d, piece_e, piece_f,
    gathered, cotangent,
    hidden, send_out, keep_out, rows_out,
    weight, tokens, turned, grads, tiles, sems,
):
    weight[...] = jnp.zeros_like(weight)
    tiles[...] = jnp.zeros_like(tiles)

    first = 0
    for piece in (piece_a, piece_b, piece_c, piece_d, piece_e, piece_f):
        count = piece.shape[0]

        def put(index, unused, piece=piece, first=first):
            slot = ranks[first + index // PER] * PER + index % PER
            for m in range(2):
                weight[place[m, slot], :, m * TILE:(m + 1) * TILE] = piece[index, m]
            return unused

        lax.fori_loop(0, count, put, 0, unroll=4)
        first += count // PER

    for z in range(ZS):
        for l in range(YL):
            tokens[l * 128 + z * 16:l * 128 + z * 16 + 16, :] = gathered[z, l]
    for r in range(0, WIDTH, 512):
        turned[r:r + 512, :] = tokens[:, r:r + 512].T

    def forward(c, unused):
        dense = weight[pl.ds(c * ROWS, ROWS)].reshape(WIDTH, 2 * TILE)
        total = jnp.dot(tokens[...], dense, preferred_element_type=jnp.float32)
        gate, up = total[:, :TILE], total[:, TILE:]
        lanes = pl.ds(pl.multiple_of(c * TILE, TILE), TILE)
        sigma = 1.0 / (1.0 + jnp.exp(-gate))
        swish = gate * sigma
        hidden[:, lanes] = (swish * up).astype(jnp.bfloat16)
        out_grad = cotangent[:, lanes].astype(jnp.float32)
        grads[c, :, TILE:] = (out_grad * swish).astype(jnp.bfloat16)
        grads[c, :, :TILE] = (
            out_grad * up * sigma * (1.0 + gate * (1.0 - sigma))
        ).astype(jnp.bfloat16)
        return unused

    lax.fori_loop(0, COLS, forward, 0)

    span = 512

    def tile_sums(step, unused):
        c = step // (WIDTH // span)
        part = step % (WIDTH // span)
        rows = pl.ds(pl.multiple_of(part * span, span), span)
        total = jnp.dot(turned[rows, :], grads[c], preferred_element_type=jnp.float32)
        total = total.astype(jnp.bfloat16)
        for i in range(span // TILE):
            for m in range(2):
                spot = target[m, (part * (span // TILE) + i) * COLS + c]
                tiles[spot, m] = total[i * TILE:(i + 1) * TILE, m * TILE:(m + 1) * TILE]
        return unused

    lax.fori_loop(0, COLS * (WIDTH // span), tile_sums, 0)
    half = CAP // 2
    first_copy = pltpu.make_async_copy(tiles.at[pl.ds(0, half)], send_out, sems.at[0])
    first_copy.start()
    second_copy = pltpu.make_async_copy(tiles.at[pl.ds(half, half)], keep_out, sems.at[1])
    second_copy.start()

    def row_sums(part, unused):
        total = jnp.zeros((GROUP, 2 * TILE), jnp.float32)
        for c in range(COLS):
            dense = weight[pl.ds(c * ROWS + part * 2, 2)].reshape(2 * TILE, 2 * TILE)
            total += lax.dot_general(
                grads[c], dense, (((1,), (1,)), ((), ())), preferred_element_type=jnp.float32
            )
        total = total.astype(jnp.bfloat16)
        lanes = pl.ds(pl.multiple_of(part * 256, 256), 256)
        for z in range(ZS):
            for l in range(YL):
                rows_out[z, l, :, lanes] = total[l * 128 + z * 16:l * 128 + z * 16 + 16]
        return unused

    lax.fori_loop(0, WIDTH // 256, row_sums, 0)
    first_copy.wait()
    second_copy.wait()


def local_work(place, target, ranks, pieces, gathered, cotangent):
    smem = pl.BlockSpec(memory_space=pltpu.SMEM)
    vmem = pl.BlockSpec(memory_space=pltpu.VMEM)
    hbm = pl.BlockSpec(memory_space=pl.ANY)
    bf16 = jnp.bfloat16
    return pl.pallas_call(
        kernel,
        out_shape=(
            jax.ShapeDtypeStruct((GROUP, HIDE), bf16),
            jax.ShapeDtypeStruct((CAP // 2, 2, TILE, TILE), bf16),
            jax.ShapeDtypeStruct((CAP // 2, 2, TILE, TILE), bf16),
            jax.ShapeDtypeStruct((ZS, YL, 16, WIDTH), bf16),
        ),
        in_specs=[smem] * 3 + [vmem] * 8,
        out_specs=(vmem, hbm, hbm, vmem),
        scratch_shapes=[
            pltpu.VMEM((DEAD + 1, TILE, 2 * TILE), bf16),
            pltpu.VMEM((GROUP, WIDTH), bf16),
            pltpu.VMEM((WIDTH, GROUP), bf16),
            pltpu.VMEM((COLS, GROUP, 2 * TILE), bf16),
            pltpu.VMEM((CAP + 1, 2, TILE, TILE), bf16),
            pltpu.SemaphoreType.DMA((2,)),
        ],
        compiler_params=pltpu.CompilerParams(vmem_limit_bytes=58 * 1024 * 1024),
        cost_estimate=pl.CostEstimate(
            flops=6 * GROUP * WIDTH * 2 * HIDE, bytes_accessed=24 << 20, transcendentals=GROUP * HIDE
        ),
        name="swiglu_local",
    )(place, target, ranks, *pieces, gathered, cotangent)


def tables(keep_local, x, y, c):
    keep = keep_local.reshape(2, ROWS * COLS)
    spots = jnp.arange(ROWS * COLS, dtype=jnp.int32)
    order = jnp.sum(jnp.where(spots[None, :] <= spots[:, None], keep[:, None, :], 0), axis=2) - 1
    dense_spot = (spots % COLS) * ROWS + spots // COLS
    slots = jnp.arange(CAP, dtype=jnp.int32)
    match = (order[:, None, :] == slots[None, :, None]) & (keep[:, None, :] == 1)
    place = DEAD + jnp.sum(jnp.where(match, dense_spot - DEAD, 0), axis=2)
    owner = order // PER
    dx = (owner // (YS * CS) - x) % XS
    dy = (owner // CS) % YS ^ y
    dc = owner % CS ^ c
    block = jnp.zeros_like(owner)
    for (a, b), at in BLOCKS.items():
        block = jnp.where((dx == a) & (dy == b), at, block)
    target = ((1 - dc) * len(BLOCKS) + block) * PER + order % PER
    target = jnp.where(keep == 1, target, CAP)
    return place.astype(jnp.int32), target.astype(jnp.int32)


def piece_ranks(x, y, c):
    spots = [(0, 0), (-1, 0), (1, 0), (0, 1), (2, 0), (-1, 1), (1, 1), (2, 1)]
    ranks = [
        (((x + dx) % XS) * YS + (y ^ dy)) * CS + (c ^ dc) for dc in range(2) for dx, dy in spots
    ]
    return jnp.stack(ranks).astype(jnp.int32)


def body(tokens, weight_tiles, keep_mask, cotangent):
    f32, bf16 = jnp.float32, jnp.bfloat16
    rank = lax.axis_index("dp")
    x, y, c = rank // (YS * CS), (rank // CS) % YS, rank % CS
    low = lax.axis_index("tensor") // ZS
    place, target = tables(keep_mask, x, y, c)
    ranks = piece_ranks(x, y, c)

    other = lax.ppermute(tokens, "tensor", L_SWAP)
    pair = jnp.where(low == 0, jnp.stack([tokens, other]), jnp.stack([other, tokens]))
    gathered = lax.all_gather(pair, "tensor", axis=0, axis_index_groups=Z_RINGS)

    own = weight_tiles[0]
    below = lax.ppermute(own, "dp", X_UP)
    above = lax.ppermute(own, "dp", X_DOWN)
    across = lax.ppermute(own, "dp", Y_SWAP)
    far_low = lax.ppermute(below[:PER // 2], "dp", X_UP)
    far_high = lax.ppermute(above[PER // 2:], "dp", X_DOWN)
    far = jnp.concatenate([far_low, far_high])
    below_across = lax.ppermute(across, "dp", X_UP)
    above_across = lax.ppermute(across, "dp", X_DOWN)
    far_across = lax.ppermute(far, "dp", Y_SWAP)
    piece_a = jnp.concatenate([own, below, above])
    piece_b = jnp.concatenate([across, far])
    piece_c = jnp.concatenate([below_across, above_across, far_across])
    pieces = [piece_a, piece_b, piece_c]
    pieces = pieces + [lax.ppermute(piece, "dp", C_SWAP) for piece in pieces]

    hidden, send, keep, rows = local_work(place, target, ranks, pieces, gathered, cotangent)

    summed = lax.psum_scatter(rows, "tensor", scatter_dimension=0, axis_index_groups=Z_RINGS)
    mine = jnp.where(low == 0, summed[0], summed[1])
    theirs = jnp.where(low == 0, summed[1], summed[0])
    back = lax.ppermute(theirs, "tensor", L_SWAP)
    grad_tokens = (mine.astype(f32) + back.astype(f32)).astype(bf16)

    came = lax.ppermute(send, "dp", C_SWAP)

    def block(dx, dy):
        at = BLOCKS[dx, dy] * PER
        return keep[at:at + PER].astype(f32) + came[at:at + PER].astype(f32)

    up_in = lax.ppermute(block(1, 1).astype(bf16), "dp", X_UP)
    down_in = lax.ppermute(block(3, 1).astype(bf16), "dp", X_DOWN)
    far_in = lax.ppermute(block(2, 1).astype(bf16), "dp", Y_SWAP)
    far_sum = (block(2, 0) + far_in.astype(f32)).astype(bf16)
    across_sum = (block(0, 1) + up_in.astype(f32) + down_in.astype(f32)).astype(bf16)
    half_up = lax.ppermute(far_sum[:PER // 2], "dp", X_UP)
    half_down = lax.ppermute(far_sum[PER // 2:], "dp", X_DOWN)
    across_in = lax.ppermute(across_sum, "dp", Y_SWAP)
    up_block, down_block = block(1, 0), block(3, 0)
    up_sum = jnp.concatenate([up_block[:PER // 2] + half_up.astype(f32), up_block[PER // 2:]])
    down_sum = jnp.concatenate([down_block[:PER // 2], down_block[PER // 2:] + half_down.astype(f32)])
    up_last = lax.ppermute(up_sum.astype(bf16), "dp", X_UP)
    down_last = lax.ppermute(down_sum.astype(bf16), "dp", X_DOWN)
    total = block(0, 0) + across_in.astype(f32) + up_last.astype(f32) + down_last.astype(f32)
    tile_grads = (total * (1.0 / (XS * YS * CS)))[None]
    return hidden, grad_tokens, tile_grads


def solution(mesh):
    in_specs = (
        P(("dp", "tensor"), None),
        P("tensor", "dp", None, None, None),
        P(None, None, "tensor"),
        P("dp", "tensor"),
    )
    out_specs = (P("dp", "tensor"), P(("dp", "tensor"), None), P("tensor", "dp", None, None, None))
    return jax.shard_map(body, mesh=mesh, in_specs=in_specs, out_specs=out_specs, check_vma=False)
```

```python
import jax
import jax.numpy as jnp
from jax import lax
from jax.experimental import pallas as pl
from jax.experimental.pallas import tpu as pltpu
from jax.sharding import PartitionSpec as P

TILE = 128
ROWS = 32
COLS = 7
CAP = 128
PER = 8
GROUP = 256
WIDTH = ROWS * TILE
HIDE = COLS * TILE
DEAD = ROWS * COLS
XS, YS, CS = 4, 2, 2
ZS, YL = 8, 2


def dp_perm(move):
    def index(x, y, c):
        return (x * YS + y) * CS + c

    return [
        (index(x, y, c), index(*move(x, y, c)))
        for x in range(XS)
        for y in range(YS)
        for c in range(CS)
    ]


X_UP = dp_perm(lambda x, y, c: ((x + 1) % XS, y, c))
X_DOWN = dp_perm(lambda x, y, c: ((x - 1) % XS, y, c))
Y_SWAP = dp_perm(lambda x, y, c: (x, 1 - y, c))
C_SWAP = dp_perm(lambda x, y, c: (x, y, 1 - c))
L_SWAP = [(l * ZS + z, (1 - l) * ZS + z) for l in range(YL) for z in range(ZS)]
Z_RINGS = [[l * ZS + z for z in range(ZS)] for l in range(YL)]

BLOCKS = {(1, 1): 0, (3, 1): 1, (2, 1): 2, (0, 1): 3, (2, 0): 4, (1, 0): 5, (3, 0): 6, (0, 0): 7}
EARLY = 3 * PER
HALF = len(BLOCKS) * PER
PIECES = 2 * len(BLOCKS)
VMEM_LIMIT = 58 * 1024 * 1024


def start_rows(low, gathered, tokens, sems):
    copies = []
    for z in range(ZS):
        for l in range(YL):
            first = pl.multiple_of((low[0] ^ l) * (GROUP // YL) + z * 16, 16)
            copies.append(
                pltpu.make_async_copy(
                    gathered.at[z, l], tokens.at[pl.ds(first, 16)], sems.at[z * YL + l]
                )
            )
            copies[-1].start()
    return copies


def dense_kernel(*refs):
    place, ranks, low = refs[:3]
    pieces = refs[3:3 + PIECES]
    gathered, cotangent, hidden, grads, rows_out = refs[3 + PIECES:8 + PIECES]
    weight, stored, tokens, rows, piece_sems, row_sems, out_sems = refs[8 + PIECES:]
    copies = []
    for p in range(PIECES):
        copies.append(
            pltpu.make_async_copy(pieces[p], stored.at[pl.ds(p * PER, PER)], piece_sems.at[p])
        )
        copies[-1].start()
    row_copies = start_rows(low, gathered, tokens, row_sems)
    weight[...] = jnp.zeros_like(weight)
    for p in range(PIECES):
        copies[p].wait()
        for j in range(PER):
            for m in range(2):
                spot = place[m, ranks[p] * PER + j]
                weight[spot, :, m * TILE:(m + 1) * TILE] = stored[p * PER + j, m]
    for copy in row_copies:
        copy.wait()

    for c in range(COLS):
        dense = weight[c * ROWS:(c + 1) * ROWS].reshape(WIDTH, 2 * TILE)
        total = jnp.dot(tokens[...], dense, preferred_element_type=jnp.float32)
        gate, up = total[:, :TILE], total[:, TILE:]
        lanes = slice(c * TILE, (c + 1) * TILE)
        sigma = 1.0 / (1.0 + jnp.exp(-gate))
        swish = gate * sigma
        hidden[:, lanes] = (swish * up).astype(jnp.bfloat16)
        out_grad = cotangent[:, lanes].astype(jnp.float32)
        grads[c, :, TILE:] = (out_grad * swish).astype(jnp.bfloat16)
        grads[c, :, :TILE] = (
            out_grad * up * sigma * (1.0 + gate * (1.0 - sigma))
        ).astype(jnp.bfloat16)

    span = 256
    out_copies = []
    for part in range(WIDTH // span):
        total = jnp.zeros((GROUP, span), jnp.float32)
        for c in range(COLS):
            dense = weight[c * ROWS + part * 2:c * ROWS + part * 2 + 2].reshape(span, 2 * TILE)
            total += lax.dot_general(
                grads[c], dense, (((1,), (1,)), ((), ())), preferred_element_type=jnp.float32
            )
        lanes = slice(part * span, (part + 1) * span)
        for z in range(ZS):
            for l in range(YL):
                rows[z, l, :, lanes] = total[l * 128 + z * 16:l * 128 + z * 16 + 16]
        if part % 4 == 3:
            wide = pl.ds((part - 3) * span, 4 * span)
            out_copies.append(
                pltpu.make_async_copy(
                    rows.at[:, :, :, wide], rows_out.at[:, :, :, wide], out_sems.at[part // 4]
                )
            )
            out_copies[-1].start()
    for copy in out_copies:
        copy.wait()


def dense_work(place, ranks, low, pieces, gathered, cotangent):
    smem = pl.BlockSpec(memory_space=pltpu.SMEM)
    vmem = pl.BlockSpec(memory_space=pltpu.VMEM)
    hbm = pl.BlockSpec(memory_space=pl.ANY)
    bf16 = jnp.bfloat16
    return pl.pallas_call(
        dense_kernel,
        out_shape=(
            jax.ShapeDtypeStruct((GROUP, HIDE), bf16),
            jax.ShapeDtypeStruct((COLS, GROUP, 2 * TILE), bf16),
            jax.ShapeDtypeStruct((ZS, YL, 16, WIDTH), jnp.float32),
        ),
        in_specs=[smem] * 3 + [hbm] * (PIECES + 1) + [vmem],
        out_specs=(vmem, vmem, hbm),
        scratch_shapes=[
            pltpu.VMEM((DEAD + 1, TILE, 2 * TILE), bf16),
            pltpu.VMEM((CAP, 2, TILE, TILE), bf16),
            pltpu.VMEM((GROUP, WIDTH), bf16),
            pltpu.VMEM((ZS, YL, 16, WIDTH), jnp.float32),
            pltpu.SemaphoreType.DMA((PIECES,)),
            pltpu.SemaphoreType.DMA((ZS * YL,)),
            pltpu.SemaphoreType.DMA((4,)),
        ],
        compiler_params=pltpu.CompilerParams(vmem_limit_bytes=VMEM_LIMIT),
        cost_estimate=pl.CostEstimate(
            flops=4 * GROUP * WIDTH * 2 * HIDE, bytes_accessed=16 << 20, transcendentals=GROUP * HIDE
        ),
        name="forward_and_rows",
    )(place, ranks, low, *pieces, gathered, cotangent)


def tile_kernel(
    target, low, gathered, grads, early_out, late_out, keep_out, tokens, turned, tiles, row_sems, sems
):
    row_copies = start_rows(low, gathered, tokens, row_sems)
    tiles[...] = jnp.zeros_like(tiles)
    for copy in row_copies:
        copy.wait()
    for r in range(0, WIDTH, 512):
        turned[r:r + 512, :] = tokens[:, r:r + 512].T
    span = 256

    def column(c, unused):
        for part in range(WIDTH // span):
            total = jnp.dot(
                turned[part * span:(part + 1) * span, :], grads[c],
                preferred_element_type=jnp.float32,
            ).astype(jnp.bfloat16)
            for i in range(span // TILE):
                for m in range(2):
                    spot = target[m, (part * (span // TILE) + i) * COLS + c]
                    tiles[spot, m] = total[i * TILE:(i + 1) * TILE, m * TILE:(m + 1) * TILE]
        return unused

    lax.fori_loop(0, COLS, column, 0)
    copies = [
        pltpu.make_async_copy(tiles.at[pl.ds(0, EARLY)], early_out, sems.at[0]),
        pltpu.make_async_copy(tiles.at[pl.ds(EARLY, HALF - EARLY)], late_out, sems.at[1]),
        pltpu.make_async_copy(tiles.at[pl.ds(HALF, HALF)], keep_out, sems.at[2]),
    ]
    for copy in copies:
        copy.start()
    for copy in copies:
        copy.wait()


def tile_work(target, low, gathered, grads):
    smem = pl.BlockSpec(memory_space=pltpu.SMEM)
    vmem = pl.BlockSpec(memory_space=pltpu.VMEM)
    hbm = pl.BlockSpec(memory_space=pl.ANY)
    bf16 = jnp.bfloat16
    return pl.pallas_call(
        tile_kernel,
        out_shape=tuple(
            jax.ShapeDtypeStruct((n, 2, TILE, TILE), bf16) for n in (EARLY, HALF - EARLY, HALF)
        ),
        in_specs=[smem] * 2 + [hbm, vmem],
        out_specs=(hbm,) * 3,
        scratch_shapes=[
            pltpu.VMEM((GROUP, WIDTH), bf16),
            pltpu.VMEM((WIDTH, GROUP), bf16),
            pltpu.VMEM((CAP + 1, 2, TILE, TILE), bf16),
            pltpu.SemaphoreType.DMA((ZS * YL,)),
            pltpu.SemaphoreType.DMA((3,)),
        ],
        compiler_params=pltpu.CompilerParams(vmem_limit_bytes=VMEM_LIMIT),
        cost_estimate=pl.CostEstimate(
            flops=2 * GROUP * WIDTH * 2 * HIDE, bytes_accessed=12 << 20, transcendentals=0
        ),
        name="tile_sums",
    )(target, low, gathered, grads)


def tables(keep_local, x, y, c):
    keep = keep_local.reshape(2, ROWS * COLS)
    spots = jnp.arange(ROWS * COLS, dtype=jnp.int32)
    order = jnp.sum(jnp.where(spots[None, :] <= spots[:, None], keep[:, None, :], 0), axis=2) - 1
    dense_spot = (spots % COLS) * ROWS + spots // COLS
    slots = jnp.arange(CAP, dtype=jnp.int32)
    match = (order[:, None, :] == slots[None, :, None]) & (keep[:, None, :] == 1)
    place = DEAD + jnp.sum(jnp.where(match, dense_spot - DEAD, 0), axis=2)
    owner = order >> 3
    dx = ((owner >> 2) - x) & (XS - 1)
    dy = ((owner >> 1) & 1) ^ y
    dc = (owner & 1) ^ c
    block = jnp.zeros_like(owner)
    for (a, b), at in BLOCKS.items():
        block = jnp.where((dx == a) & (dy == b), at, block)
    target = ((1 - dc) * len(BLOCKS) + block) * PER + (order & (PER - 1))
    target = jnp.where(keep == 1, target, CAP)
    return place.astype(jnp.int32), target.astype(jnp.int32)


def piece_ranks(x, y, c):
    spots = [(0, 0), (3, 0), (1, 0), (0, 1), (2, 0), (3, 1), (1, 1), (2, 1)]
    dx = jnp.array([a for a, b in spots] * 2, jnp.int32)
    dy = jnp.array([b for a, b in spots] * 2, jnp.int32)
    dc = jnp.array([0] * len(spots) + [1] * len(spots), jnp.int32)
    return (((x + dx) & (XS - 1)) * YS + (y ^ dy)) * CS + (c ^ dc)


def body(tokens, weight_tiles, keep_mask, cotangent):
    f32, bf16 = jnp.float32, jnp.bfloat16
    rank = lax.axis_index("dp")
    x, y, c = rank >> 2, (rank >> 1) & 1, rank & 1
    low = lax.axis_index("tensor") >> 3

    other = lax.ppermute(tokens, "tensor", L_SWAP)
    own = weight_tiles[0]
    below = lax.ppermute(own, "dp", X_UP)
    above = lax.ppermute(own, "dp", X_DOWN)
    across = lax.ppermute(own, "dp", Y_SWAP)
    gathered = lax.all_gather(
        jnp.stack([tokens, other]), "tensor", axis=0, axis_index_groups=Z_RINGS
    )
    place, target = tables(keep_mask, x, y, c)
    ranks = piece_ranks(x, y, c)
    half = PER // 2
    far_low = lax.ppermute(below[:half], "dp", X_UP)
    far_high = lax.ppermute(above[half:], "dp", X_DOWN)
    far = jnp.concatenate([far_low, far_high])
    below_across = lax.ppermute(across, "dp", X_UP)
    above_across = lax.ppermute(across, "dp", X_DOWN)
    far_across = lax.ppermute(far, "dp", Y_SWAP)
    pieces = [own, below, above, across, far, below_across, above_across, far_across]
    pieces = pieces + [lax.ppermute(piece, "dp", C_SWAP) for piece in pieces]
    low_table = low.reshape(1).astype(jnp.int32)

    hidden, grads, rows = dense_work(place, ranks, low_table, pieces, gathered, cotangent)
    summed = lax.psum_scatter(rows, "tensor", scatter_dimension=0, axis_index_groups=Z_RINGS)
    early, late, keep = tile_work(target, low_table, gathered, grads)

    early_in = lax.ppermute(early, "dp", C_SWAP)

    def block(dx, dy, late_in=None):
        at = BLOCKS[dx, dy] * PER
        came = early_in[at:at + PER] if at < EARLY else late_in[at - EARLY:at - EARLY + PER]
        return keep[at:at + PER].astype(f32) + came.astype(f32)

    sends = [block(*at).astype(bf16) for at in ((2, 1), (1, 1), (3, 1))]
    *sends, late = lax.optimization_barrier((*sends, late))
    far_in = lax.ppermute(sends[0], "dp", Y_SWAP)
    up_in = lax.ppermute(sends[1], "dp", X_UP)
    down_in = lax.ppermute(sends[2], "dp", X_DOWN)
    late_in = lax.ppermute(late, "dp", C_SWAP)
    far_in, up_in, down_in, late_one = lax.optimization_barrier((far_in, up_in, down_in, late_in))
    far_sum = block(2, 0, late_one) + far_in.astype(f32)
    across_sum = block(0, 1, late_one) + up_in.astype(f32) + down_in.astype(f32)
    sends = lax.optimization_barrier(
        (across_sum.astype(bf16), far_sum[:half].astype(bf16), far_sum[half:].astype(bf16))
    )
    across_in = lax.ppermute(sends[0], "dp", Y_SWAP)
    half_up = lax.ppermute(sends[1], "dp", X_UP)
    half_down = lax.ppermute(sends[2], "dp", X_DOWN)
    half_up, half_down, late_two = lax.optimization_barrier((half_up, half_down, late_one))
    none = jnp.zeros_like(half_up)
    up_sum = block(1, 0, late_two) + jnp.concatenate([half_up, none]).astype(f32)
    down_sum = block(3, 0, late_two) + jnp.concatenate([none, half_down]).astype(f32)
    sends = lax.optimization_barrier((up_sum.astype(bf16), down_sum.astype(bf16)))
    up_last = lax.ppermute(sends[0], "dp", X_UP)
    down_last = lax.ppermute(sends[1], "dp", X_DOWN)
    up_last, down_last, across_in, late_three = lax.optimization_barrier(
        (up_last, down_last, across_in, late_two)
    )
    total = block(0, 0, late_three) + across_in.astype(f32)
    total = total + up_last.astype(f32) + down_last.astype(f32)
    tile_grads = (total * (1.0 / (XS * YS * CS)))[None]

    mine = jnp.where(low == 0, summed[0], summed[1])
    theirs = jnp.where(low == 0, summed[1], summed[0])
    back = lax.ppermute(theirs.astype(bf16), "tensor", L_SWAP)
    grad_tokens = (mine + back.astype(f32)).astype(bf16)
    return hidden, grad_tokens, tile_grads


def solution(mesh):
    in_specs = (
        P(("dp", "tensor"), None),
        P("tensor", "dp", None, None, None),
        P(None, None, "tensor"),
        P("dp", "tensor"),
    )
    out_specs = (P("dp", "tensor"), P(("dp", "tensor"), None), P("tensor", "dp", None, None, None))
    return jax.shard_map(body, mesh=mesh, in_specs=in_specs, out_specs=out_specs, check_vma=False)
```

```python
import jax
import jax.numpy as jnp
from jax import lax
from jax.experimental import pallas as pl
from jax.experimental.pallas import tpu as pltpu
from jax.sharding import PartitionSpec as P

TILE = 128
ROWS = 32
COLS = 7
CAP = 128
PER = 8
GROUP = 256
WIDTH = ROWS * TILE
HIDE = COLS * TILE
DEAD = ROWS * COLS
XS, YS, CS = 4, 2, 2
ZS, YL = 8, 2


def dp_perm(move):
    def index(x, y, c):
        return (x * YS + y) * CS + c

    return [
        (index(x, y, c), index(*move(x, y, c)))
        for x in range(XS)
        for y in range(YS)
        for c in range(CS)
    ]


X_UP = dp_perm(lambda x, y, c: ((x + 1) % XS, y, c))
X_DOWN = dp_perm(lambda x, y, c: ((x - 1) % XS, y, c))
Y_SWAP = dp_perm(lambda x, y, c: (x, 1 - y, c))
C_SWAP = dp_perm(lambda x, y, c: (x, y, 1 - c))
L_SWAP = [(l * ZS + z, (1 - l) * ZS + z) for l in range(YL) for z in range(ZS)]


def z_perm(step):
    return [(l * ZS + z, l * ZS + (z + step) % ZS) for l in range(YL) for z in range(ZS)]


BLOCKS = {(1, 1): 0, (3, 1): 1, (2, 1): 2, (0, 1): 3, (2, 0): 4, (1, 0): 5, (3, 0): 6, (0, 0): 7}
EARLY = 3 * PER
HALF = len(BLOCKS) * PER
PIECES = 2 * len(BLOCKS)
VMEM_LIMIT = 58 * 1024 * 1024


PAIRS = [((0,), (0, 1)), ((6,), (0, 1)), ((2,), (0, 1)), ((7, 5), (0, 1)), ((1, 3), (0, 1)), ((4,), (0,)), ((4,), (1,))]
SUMS = [((0,), (0, 1)), ((2,), (0, 1)), ((6,), (0, 1)), ((1, 3), (0, 1)), ((7, 5), (0, 1)), ((4,), (0,)), ((4,), (1,))]
LINE = 16


def row_start(here, dz, l):
    return pl.multiple_of((here[0] ^ l) * (GROUP // YL) + ((here[1] + dz) & (ZS - 1)) * LINE, LINE)


def dense_kernel(*refs):
    place, ranks, here = refs[:3]
    pieces = refs[3:3 + PIECES]
    pairs = refs[3 + PIECES:3 + PIECES + len(PAIRS)]
    refs = refs[3 + PIECES + len(PAIRS):]
    cotangent, hidden, grads, tokens_out = refs[:4]
    rows_out = refs[4:4 + len(SUMS)]
    weight, stored, tokens, rows, piece_sems, row_sems, out_sems = refs[4 + len(SUMS):]
    copies = []
    for p in range(PIECES):
        copies.append(
            pltpu.make_async_copy(pieces[p], stored.at[pl.ds(p * PER, PER)], piece_sems.at[p])
        )
        copies[-1].start()
    row_copies = []
    for pair, (distances, parts) in zip(pairs, PAIRS):
        for i, dz in enumerate(distances):
            for j, l in enumerate(parts):
                row_copies.append(
                    pltpu.make_async_copy(
                        pair.at[i, j],
                        tokens.at[pl.ds(row_start(here, dz, l), LINE)],
                        row_sems.at[len(row_copies)],
                    )
                )
                row_copies[-1].start()
    weight[...] = jnp.zeros_like(weight)
    for p in range(PIECES):
        copies[p].wait()
        for j in range(PER):
            for m in range(2):
                spot = place[m, ranks[p] * PER + j]
                weight[spot, :, m * TILE:(m + 1) * TILE] = stored[p * PER + j, m]
    for copy in row_copies:
        copy.wait()
    out_copies = [pltpu.make_async_copy(tokens, tokens_out, out_sems.at[ZS * YL])]
    out_copies[0].start()

    for c in range(COLS):
        dense = weight[c * ROWS:(c + 1) * ROWS].reshape(WIDTH, 2 * TILE)
        total = jnp.dot(tokens[...], dense, preferred_element_type=jnp.float32)
        gate, up = total[:, :TILE], total[:, TILE:]
        lanes = slice(c * TILE, (c + 1) * TILE)
        sigma = 1.0 / (1.0 + jnp.exp(-gate))
        swish = gate * sigma
        hidden[:, lanes] = (swish * up).astype(jnp.bfloat16)
        out_grad = cotangent[:, lanes].astype(jnp.float32)
        grads[c, :, TILE:] = (out_grad * swish).astype(jnp.bfloat16)
        grads[c, :, :TILE] = (
            out_grad * up * sigma * (1.0 + gate * (1.0 - sigma))
        ).astype(jnp.bfloat16)

    span = 256
    for part in range(WIDTH // span):
        total = jnp.zeros((GROUP, span), jnp.float32)
        for c in range(COLS):
            dense = weight[c * ROWS + part * 2:c * ROWS + part * 2 + 2].reshape(span, 2 * TILE)
            total += lax.dot_general(
                grads[c], dense, (((1,), (1,)), ((), ())), preferred_element_type=jnp.float32
            )
        total = total.astype(jnp.bfloat16)
        lanes = slice(part * span, (part + 1) * span)
        for z in range(ZS):
            dz = (z - here[1]) & (ZS - 1)
            for l in range(YL):
                first = l * (GROUP // YL) + z * LINE
                rows[dz, l ^ here[0], :, lanes] = total[first:first + LINE]
    for out, (distances, parts) in zip(rows_out, SUMS):
        for i, dz in enumerate(distances):
            for j, l in enumerate(parts):
                out_copies.append(
                    pltpu.make_async_copy(
                        rows.at[dz, l], out.at[i, j], out_sems.at[len(out_copies) - 1]
                    )
                )
                out_copies[-1].start()
    for copy in out_copies:
        copy.wait()


def dense_work(place, ranks, here, pieces, pairs, cotangent):
    smem = pl.BlockSpec(memory_space=pltpu.SMEM)
    vmem = pl.BlockSpec(memory_space=pltpu.VMEM)
    hbm = pl.BlockSpec(memory_space=pl.ANY)
    bf16 = jnp.bfloat16
    return pl.pallas_call(
        dense_kernel,
        out_shape=(
            jax.ShapeDtypeStruct((GROUP, HIDE), bf16),
            jax.ShapeDtypeStruct((COLS, GROUP, 2 * TILE), bf16),
            jax.ShapeDtypeStruct((GROUP, WIDTH), bf16),
        )
        + tuple(jax.ShapeDtypeStruct((len(d), len(l), LINE, WIDTH), bf16) for d, l in SUMS),
        in_specs=[smem] * 3 + [hbm] * (PIECES + len(PAIRS)) + [vmem],
        out_specs=(vmem, vmem) + (hbm,) * (1 + len(SUMS)),
        scratch_shapes=[
            pltpu.VMEM((DEAD + 1, TILE, 2 * TILE), bf16),
            pltpu.VMEM((CAP, 2, TILE, TILE), bf16),
            pltpu.VMEM((GROUP, WIDTH), bf16),
            pltpu.VMEM((ZS, YL, LINE, WIDTH), bf16),
            pltpu.SemaphoreType.DMA((PIECES,)),
            pltpu.SemaphoreType.DMA((ZS * YL,)),
            pltpu.SemaphoreType.DMA((ZS * YL + 1,)),
        ],
        compiler_params=pltpu.CompilerParams(vmem_limit_bytes=VMEM_LIMIT),
        cost_estimate=pl.CostEstimate(
            flops=4 * GROUP * WIDTH * 2 * HIDE, bytes_accessed=16 << 20, transcendentals=GROUP * HIDE
        ),
        name="forward_and_rows",
    )(place, ranks, here, *pieces, *pairs, cotangent)


def tile_kernel(
    target, tokens_in, grads, early_out, late_out, keep_out, tokens, turned, tiles, sems
):
    copy = pltpu.make_async_copy(tokens_in, tokens, sems.at[3])
    copy.start()
    tiles[...] = jnp.zeros_like(tiles)
    copy.wait()
    for r in range(0, WIDTH, 512):
        turned[r:r + 512, :] = tokens[:, r:r + 512].T
    span = 256

    def column(c, unused):
        for part in range(WIDTH // span):
            total = jnp.dot(
                turned[part * span:(part + 1) * span, :], grads[c],
                preferred_element_type=jnp.float32,
            ).astype(jnp.bfloat16)
            for i in range(span // TILE):
                for m in range(2):
                    spot = target[m, (part * (span // TILE) + i) * COLS + c]
                    tiles[spot, m] = total[i * TILE:(i + 1) * TILE, m * TILE:(m + 1) * TILE]
        return unused

    lax.fori_loop(0, COLS, column, 0)
    copies = [
        pltpu.make_async_copy(tiles.at[pl.ds(0, EARLY)], early_out, sems.at[0]),
        pltpu.make_async_copy(tiles.at[pl.ds(EARLY, HALF - EARLY)], late_out, sems.at[1]),
        pltpu.make_async_copy(tiles.at[pl.ds(HALF, HALF)], keep_out, sems.at[2]),
    ]
    for copy in copies:
        copy.start()
    for copy in copies:
        copy.wait()


def tile_work(target, tokens, grads):
    smem = pl.BlockSpec(memory_space=pltpu.SMEM)
    vmem = pl.BlockSpec(memory_space=pltpu.VMEM)
    hbm = pl.BlockSpec(memory_space=pl.ANY)
    bf16 = jnp.bfloat16
    return pl.pallas_call(
        tile_kernel,
        out_shape=tuple(
            jax.ShapeDtypeStruct((n, 2, TILE, TILE), bf16) for n in (EARLY, HALF - EARLY, HALF)
        ),
        in_specs=[smem, hbm, vmem],
        out_specs=(hbm,) * 3,
        scratch_shapes=[
            pltpu.VMEM((GROUP, WIDTH), bf16),
            pltpu.VMEM((WIDTH, GROUP), bf16),
            pltpu.VMEM((CAP + 1, 2, TILE, TILE), bf16),
            pltpu.SemaphoreType.DMA((4,)),
        ],
        compiler_params=pltpu.CompilerParams(vmem_limit_bytes=VMEM_LIMIT),
        cost_estimate=pl.CostEstimate(
            flops=2 * GROUP * WIDTH * 2 * HIDE, bytes_accessed=12 << 20, transcendentals=0
        ),
        name="tile_sums",
    )(target, tokens, grads)


def tables(keep_local, x, y, c):
    keep = keep_local.reshape(2, ROWS * COLS)
    spots = jnp.arange(ROWS * COLS, dtype=jnp.int32)
    order = jnp.sum(jnp.where(spots[None, :] <= spots[:, None], keep[:, None, :], 0), axis=2) - 1
    dense_spot = (spots % COLS) * ROWS + spots // COLS
    slots = jnp.arange(CAP, dtype=jnp.int32)
    match = (order[:, None, :] == slots[None, :, None]) & (keep[:, None, :] == 1)
    place = DEAD + jnp.sum(jnp.where(match, dense_spot - DEAD, 0), axis=2)
    owner = order >> 3
    dx = ((owner >> 2) - x) & (XS - 1)
    dy = ((owner >> 1) & 1) ^ y
    dc = (owner & 1) ^ c
    block = jnp.zeros_like(owner)
    for (a, b), at in BLOCKS.items():
        block = jnp.where((dx == a) & (dy == b), at, block)
    target = ((1 - dc) * len(BLOCKS) + block) * PER + (order & (PER - 1))
    target = jnp.where(keep == 1, target, CAP)
    return place.astype(jnp.int32), target.astype(jnp.int32)


def piece_ranks(x, y, c):
    spots = [(0, 0), (3, 0), (1, 0), (0, 1), (2, 0), (3, 1), (1, 1), (2, 1)]
    dx = jnp.array([a for a, b in spots] * 2, jnp.int32)
    dy = jnp.array([b for a, b in spots] * 2, jnp.int32)
    dc = jnp.array([0] * len(spots) + [1] * len(spots), jnp.int32)
    return (((x + dx) & (XS - 1)) * YS + (y ^ dy)) * CS + (c ^ dc)


def body(tokens, weight_tiles, keep_mask, cotangent):
    f32, bf16 = jnp.float32, jnp.bfloat16
    rank = lax.axis_index("dp")
    x, y, c = rank >> 2, (rank >> 1) & 1, rank & 1
    line = lax.axis_index("tensor")
    here = jnp.stack([line >> 3, line & (ZS - 1)]).astype(jnp.int32)

    def shift(array, step):
        return lax.ppermute(array, "tensor", z_perm(step))

    other = lax.ppermute(tokens, "tensor", L_SWAP)
    own = weight_tiles[0]
    below = lax.ppermute(own, "dp", X_UP)
    above = lax.ppermute(own, "dp", X_DOWN)
    across = lax.ppermute(own, "dp", Y_SWAP)
    pair = jnp.stack([tokens, other])[None]
    two_below, two_above = shift(pair, 2), shift(pair, -2)
    pairs = [
        pair, two_below, two_above,
        shift(jnp.concatenate([pair, two_below]), 1), shift(jnp.concatenate([pair, two_above]), -1),
        shift(two_below[:, :1], 2), shift(two_above[:, 1:], -2),
    ]
    place, target = tables(keep_mask, x, y, c)
    ranks = piece_ranks(x, y, c)
    half = PER // 2
    far_low = lax.ppermute(below[:half], "dp", X_UP)
    far_high = lax.ppermute(above[half:], "dp", X_DOWN)
    far_low, far_high, across = lax.optimization_barrier((far_low, far_high, across))
    far = jnp.concatenate([far_low, far_high])
    below_across = lax.ppermute(across, "dp", X_UP)
    above_across = lax.ppermute(across, "dp", X_DOWN)
    far_across = lax.ppermute(far, "dp", Y_SWAP)
    pieces = [own, below, above, across, far, below_across, above_across, far_across]
    pieces = pieces + [lax.ppermute(piece, "dp", C_SWAP) for piece in pieces]

    hidden, grads, ordered, *rows = dense_work(place, ranks, here, pieces, pairs, cotangent)
    near_up, near_down = shift(rows[3], 1), shift(rows[4], -1)
    four_up, four_down = shift(rows[5], 2), shift(rows[6], -2)
    early, late, keep = tile_work(target, ordered, grads)
    gap = jnp.zeros_like(four_up[0])
    two_up = rows[1][0].astype(f32) + near_up[1].astype(f32)
    two_up = two_up + jnp.concatenate([four_up[0], gap]).astype(f32)
    two_down = rows[2][0].astype(f32) + near_down[1].astype(f32)
    two_down = two_down + jnp.concatenate([gap, four_down[0]]).astype(f32)
    two_up, two_down = lax.optimization_barrier((two_up.astype(bf16), two_down.astype(bf16)))
    two_in_up, two_in_down = shift(two_up, 2), shift(two_down, -2)

    early_in = lax.ppermute(early, "dp", C_SWAP)

    def block(dx, dy, late_in=None):
        at = BLOCKS[dx, dy] * PER
        came = early_in[at:at + PER] if at < EARLY else late_in[at - EARLY:at - EARLY + PER]
        return keep[at:at + PER].astype(f32) + came.astype(f32)

    sends = [block(*at).astype(bf16) for at in ((2, 1), (1, 1), (3, 1))]
    *sends, late = lax.optimization_barrier((*sends, late))
    far_in = lax.ppermute(sends[0], "dp", Y_SWAP)
    up_in = lax.ppermute(sends[1], "dp", X_UP)
    down_in = lax.ppermute(sends[2], "dp", X_DOWN)
    late_in = lax.ppermute(late, "dp", C_SWAP)
    far_in, up_in, down_in, late_one = lax.optimization_barrier((far_in, up_in, down_in, late_in))
    far_sum = block(2, 0, late_one) + far_in.astype(f32)
    across_sum = block(0, 1, late_one) + up_in.astype(f32) + down_in.astype(f32)
    sends = lax.optimization_barrier(
        (across_sum.astype(bf16), far_sum[:half].astype(bf16), far_sum[half:].astype(bf16))
    )
    across_in = lax.ppermute(sends[0], "dp", Y_SWAP)
    half_up = lax.ppermute(sends[1], "dp", X_UP)
    half_down = lax.ppermute(sends[2], "dp", X_DOWN)
    half_up, half_down, late_two = lax.optimization_barrier((half_up, half_down, late_one))
    none = jnp.zeros_like(half_up)
    up_sum = block(1, 0, late_two) + jnp.concatenate([half_up, none]).astype(f32)
    down_sum = block(3, 0, late_two) + jnp.concatenate([none, half_down]).astype(f32)
    sends = lax.optimization_barrier((up_sum.astype(bf16), down_sum.astype(bf16)))
    up_last = lax.ppermute(sends[0], "dp", X_UP)
    down_last = lax.ppermute(sends[1], "dp", X_DOWN)
    up_last, down_last, across_in, late_three = lax.optimization_barrier(
        (up_last, down_last, across_in, late_two)
    )
    total = block(0, 0, late_three) + across_in.astype(f32)
    total = total + up_last.astype(f32) + down_last.astype(f32)
    tile_grads = (total * (1.0 / (XS * YS * CS)))[None]

    arrived = [rows[0][0], near_up[0], near_down[0], two_in_up, two_in_down]
    theirs = sum(part[1].astype(f32) for part in arrived).astype(bf16)
    back = lax.ppermute(theirs, "tensor", L_SWAP)
    grad_tokens = sum(part[0].astype(f32) for part in arrived) + back.astype(f32)
    grad_tokens = grad_tokens.astype(bf16)
    return hidden, grad_tokens, tile_grads


def solution(mesh):
    in_specs = (
        P(("dp", "tensor"), None),
        P("tensor", "dp", None, None, None),
        P(None, None, "tensor"),
        P("dp", "tensor"),
    )
    out_specs = (P("dp", "tensor"), P(("dp", "tensor"), None), P("tensor", "dp", None, None, None))
    return jax.shard_map(body, mesh=mesh, in_specs=in_specs, out_specs=out_specs, check_vma=False)
```

```python
import jax
import jax.numpy as jnp
from jax import lax
from jax.experimental import pallas as pl
from jax.experimental.pallas import tpu as pltpu
from jax.sharding import PartitionSpec as P

TILE = 128
ROWS = 32
COLS = 7
CAP = 128
PER = 8
GROUP = 256
WIDTH = ROWS * TILE
HIDE = COLS * TILE
DEAD = ROWS * COLS
XS, YS, CS = 4, 2, 2
ZS, YL = 8, 2


def dp_perm(move):
    def index(x, y, c):
        return (x * YS + y) * CS + c

    return [
        (index(x, y, c), index(*move(x, y, c)))
        for x in range(XS)
        for y in range(YS)
        for c in range(CS)
    ]


X_UP = dp_perm(lambda x, y, c: ((x + 1) % XS, y, c))
X_DOWN = dp_perm(lambda x, y, c: ((x - 1) % XS, y, c))
Y_SWAP = dp_perm(lambda x, y, c: (x, 1 - y, c))
C_SWAP = dp_perm(lambda x, y, c: (x, y, 1 - c))
L_SWAP = [(l * ZS + z, (1 - l) * ZS + z) for l in range(YL) for z in range(ZS)]


def z_perm(step):
    return [(l * ZS + z, l * ZS + (z + step) % ZS) for l in range(YL) for z in range(ZS)]


BLOCKS = {(1, 1): 0, (3, 1): 1, (2, 1): 2, (0, 1): 3, (2, 0): 4, (1, 0): 5, (3, 0): 6, (0, 0): 7}
HALF = len(BLOCKS) * PER
PIECES = 2 * len(BLOCKS)
VMEM_LIMIT = 58 * 1024 * 1024


LINES_IN = [
    [(0, 0), (0, 1)],
    [(5, 0), (5, 1)],
    [(3, 0), (3, 1)],
    [(7, 0), (7, 1), (2, 0), (2, 1), (4, 0)],
    [(1, 0), (1, 1), (6, 0), (6, 1), (4, 1)],
]
LINES_OUT = [
    [(0, 0), (0, 1)],
    [(3, 0), (3, 1)],
    [(5, 0), (5, 1)],
    [(1, 0), (1, 1), (6, 0), (6, 1), (4, 0)],
    [(7, 0), (7, 1), (2, 0), (2, 1), (4, 1)],
]
LINE = 16


def row_start(here, dz, l):
    return pl.multiple_of((here[0] ^ l) * (GROUP // YL) + ((here[1] + dz) & (ZS - 1)) * LINE, LINE)


def dense_kernel(*refs):
    place, ranks, here = refs[:3]
    pieces = refs[3:3 + PIECES]
    pairs = refs[3 + PIECES:3 + PIECES + len(LINES_IN)]
    refs = refs[3 + PIECES + len(LINES_IN):]
    cotangent, hidden, grads, tokens_out = refs[:4]
    rows_out = refs[4:4 + len(LINES_OUT)]
    weight, stored, tokens, rows, piece_sems, row_sems, out_sems = refs[4 + len(LINES_OUT):]
    copies = []
    for p in range(PIECES):
        copies.append(
            pltpu.make_async_copy(pieces[p], stored.at[pl.ds(p * PER, PER)], piece_sems.at[p])
        )
        copies[-1].start()
    row_copies = []
    for pair, lines in zip(pairs, LINES_IN):
        for i, (dz, l) in enumerate(lines):
            row_copies.append(
                pltpu.make_async_copy(
                    pair.at[i],
                    tokens.at[pl.ds(row_start(here, dz, l), LINE)],
                    row_sems.at[len(row_copies)],
                )
            )
            row_copies[-1].start()
    weight[...] = jnp.zeros_like(weight)
    for p in range(PIECES):
        copies[p].wait()
        for j in range(PER):
            for m in range(2):
                spot = place[m, ranks[p] * PER + j]
                weight[spot, :, m * TILE:(m + 1) * TILE] = stored[p * PER + j, m]
    for copy in row_copies:
        copy.wait()
    out_copies = [pltpu.make_async_copy(tokens, tokens_out, out_sems.at[ZS * YL])]
    out_copies[0].start()

    for c in range(COLS):
        dense = weight[c * ROWS:(c + 1) * ROWS].reshape(WIDTH, 2 * TILE)
        total = jnp.dot(tokens[...], dense, preferred_element_type=jnp.float32)
        gate, up = total[:, :TILE], total[:, TILE:]
        lanes = slice(c * TILE, (c + 1) * TILE)
        sigma = 1.0 / (1.0 + jnp.exp(-gate))
        swish = gate * sigma
        hidden[:, lanes] = (swish * up).astype(jnp.bfloat16)
        out_grad = cotangent[:, lanes].astype(jnp.float32)
        grads[c, :, TILE:] = (out_grad * swish).astype(jnp.bfloat16)
        grads[c, :, :TILE] = (
            out_grad * up * sigma * (1.0 + gate * (1.0 - sigma))
        ).astype(jnp.bfloat16)

    span = 256
    for part in range(WIDTH // span):
        total = jnp.zeros((GROUP, span), jnp.float32)
        for c in range(COLS):
            dense = weight[c * ROWS + part * 2:c * ROWS + part * 2 + 2].reshape(span, 2 * TILE)
            total += lax.dot_general(
                grads[c], dense, (((1,), (1,)), ((), ())), preferred_element_type=jnp.float32
            )
        total = total.astype(jnp.bfloat16)
        lanes = slice(part * span, (part + 1) * span)
        for z in range(ZS):
            dz = (z - here[1]) & (ZS - 1)
            for l in range(YL):
                first = l * (GROUP // YL) + z * LINE
                rows[dz, l ^ here[0], :, lanes] = total[first:first + LINE]
    for out, lines in zip(rows_out, LINES_OUT):
        for i, (dz, l) in enumerate(lines):
            out_copies.append(
                pltpu.make_async_copy(rows.at[dz, l], out.at[i], out_sems.at[len(out_copies) - 1])
            )
            out_copies[-1].start()
    for copy in out_copies:
        copy.wait()


def dense_work(place, ranks, here, pieces, pairs, cotangent):
    smem = pl.BlockSpec(memory_space=pltpu.SMEM)
    vmem = pl.BlockSpec(memory_space=pltpu.VMEM)
    hbm = pl.BlockSpec(memory_space=pl.ANY)
    bf16 = jnp.bfloat16
    return pl.pallas_call(
        dense_kernel,
        out_shape=(
            jax.ShapeDtypeStruct((GROUP, HIDE), bf16),
            jax.ShapeDtypeStruct((COLS, GROUP, 2 * TILE), bf16),
            jax.ShapeDtypeStruct((GROUP, WIDTH), bf16),
        )
        + tuple(jax.ShapeDtypeStruct((len(lines), LINE, WIDTH), bf16) for lines in LINES_OUT),
        in_specs=[smem] * 3 + [hbm] * (PIECES + len(LINES_IN)) + [vmem],
        out_specs=(vmem, vmem) + (hbm,) * (1 + len(LINES_OUT)),
        scratch_shapes=[
            pltpu.VMEM((DEAD + 1, TILE, 2 * TILE), bf16),
            pltpu.VMEM((CAP, 2, TILE, TILE), bf16),
            pltpu.VMEM((GROUP, WIDTH), bf16),
            pltpu.VMEM((ZS, YL, LINE, WIDTH), bf16),
            pltpu.SemaphoreType.DMA((PIECES,)),
            pltpu.SemaphoreType.DMA((ZS * YL,)),
            pltpu.SemaphoreType.DMA((ZS * YL + 1,)),
        ],
        compiler_params=pltpu.CompilerParams(vmem_limit_bytes=VMEM_LIMIT),
        cost_estimate=pl.CostEstimate(
            flops=4 * GROUP * WIDTH * 2 * HIDE, bytes_accessed=16 << 20, transcendentals=GROUP * HIDE
        ),
        name="forward_and_rows",
    )(place, ranks, here, *pieces, *pairs, cotangent)


def tile_kernel(
    target, tokens_in, grads, send_out, keep_out, tokens, turned, tiles, sems
):
    copy = pltpu.make_async_copy(tokens_in, tokens, sems.at[2])
    copy.start()
    tiles[...] = jnp.zeros_like(tiles)
    copy.wait()
    for r in range(0, WIDTH, 512):
        turned[r:r + 512, :] = tokens[:, r:r + 512].T
    span = 256

    def column(c, unused):
        for part in range(WIDTH // span):
            total = jnp.dot(
                turned[part * span:(part + 1) * span, :], grads[c],
                preferred_element_type=jnp.float32,
            ).astype(jnp.bfloat16)
            for i in range(span // TILE):
                for m in range(2):
                    spot = target[m, (part * (span // TILE) + i) * COLS + c]
                    tiles[spot, m] = total[i * TILE:(i + 1) * TILE, m * TILE:(m + 1) * TILE]
        return unused

    lax.fori_loop(0, COLS, column, 0)
    copies = [
        pltpu.make_async_copy(tiles.at[pl.ds(0, HALF)], send_out, sems.at[0]),
        pltpu.make_async_copy(tiles.at[pl.ds(HALF, HALF)], keep_out, sems.at[1]),
    ]
    for copy in copies:
        copy.start()
    for copy in copies:
        copy.wait()


def tile_work(target, tokens, grads):
    smem = pl.BlockSpec(memory_space=pltpu.SMEM)
    vmem = pl.BlockSpec(memory_space=pltpu.VMEM)
    hbm = pl.BlockSpec(memory_space=pl.ANY)
    bf16 = jnp.bfloat16
    return pl.pallas_call(
        tile_kernel,
        out_shape=(jax.ShapeDtypeStruct((HALF, 2, TILE, TILE), bf16),) * 2,
        in_specs=[smem, hbm, vmem],
        out_specs=(hbm,) * 2,
        scratch_shapes=[
            pltpu.VMEM((GROUP, WIDTH), bf16),
            pltpu.VMEM((WIDTH, GROUP), bf16),
            pltpu.VMEM((CAP + 1, 2, TILE, TILE), bf16),
            pltpu.SemaphoreType.DMA((3,)),
        ],
        compiler_params=pltpu.CompilerParams(vmem_limit_bytes=VMEM_LIMIT),
        cost_estimate=pl.CostEstimate(
            flops=2 * GROUP * WIDTH * 2 * HIDE, bytes_accessed=12 << 20, transcendentals=0
        ),
        name="tile_sums",
    )(target, tokens, grads)


def tables(keep_local, x, y, c):
    keep = keep_local.reshape(2, ROWS * COLS)
    spots = jnp.arange(ROWS * COLS, dtype=jnp.int32)
    order = jnp.sum(jnp.where(spots[None, :] <= spots[:, None], keep[:, None, :], 0), axis=2) - 1
    dense_spot = (spots % COLS) * ROWS + spots // COLS
    slots = jnp.arange(CAP, dtype=jnp.int32)
    match = (order[:, None, :] == slots[None, :, None]) & (keep[:, None, :] == 1)
    place = DEAD + jnp.sum(jnp.where(match, dense_spot - DEAD, 0), axis=2)
    owner = order >> 3
    dx = ((owner >> 2) - x) & (XS - 1)
    dy = ((owner >> 1) & 1) ^ y
    dc = (owner & 1) ^ c
    block = jnp.zeros_like(owner)
    for (a, b), at in BLOCKS.items():
        block = jnp.where((dx == a) & (dy == b), at, block)
    target = ((1 - dc) * len(BLOCKS) + block) * PER + (order & (PER - 1))
    target = jnp.where(keep == 1, target, CAP)
    return place.astype(jnp.int32), target.astype(jnp.int32)


def piece_ranks(x, y, c):
    spots = [(0, 0), (3, 0), (1, 0), (0, 1), (2, 0), (3, 1), (1, 1), (2, 1)]
    dx = jnp.array([a for a, b in spots] * 2, jnp.int32)
    dy = jnp.array([b for a, b in spots] * 2, jnp.int32)
    dc = jnp.array([0] * len(spots) + [1] * len(spots), jnp.int32)
    return (((x + dx) & (XS - 1)) * YS + (y ^ dy)) * CS + (c ^ dc)


def body(tokens, weight_tiles, keep_mask, cotangent):
    f32, bf16 = jnp.float32, jnp.bfloat16
    rank = lax.axis_index("dp")
    x, y, c = rank >> 2, (rank >> 1) & 1, rank & 1
    line = lax.axis_index("tensor")
    here = jnp.stack([line >> 3, line & (ZS - 1)]).astype(jnp.int32)

    def shift(array, step):
        return lax.ppermute(array, "tensor", z_perm(step))

    other = lax.ppermute(tokens, "tensor", L_SWAP)
    own = weight_tiles[0]
    below = lax.ppermute(own, "dp", X_UP)
    above = lax.ppermute(own, "dp", X_DOWN)
    across = lax.ppermute(own, "dp", Y_SWAP)
    pair = jnp.stack([tokens, other])
    own, below, above, pair_one = lax.optimization_barrier((own, below, above, pair))
    three_below, three_above = shift(pair, 3), shift(pair, -3)
    place, target = tables(keep_mask, x, y, c)
    ranks = piece_ranks(x, y, c)
    half = PER // 2
    far_low = lax.ppermute(below[:half], "dp", X_UP)
    far_high = lax.ppermute(above[half:], "dp", X_DOWN)
    first = [own, below, above, across]
    mates = [lax.ppermute(piece, "dp", C_SWAP) for piece in first]
    far_low, far_high, across, three_below, three_above, *mates = lax.optimization_barrier(
        (far_low, far_high, across, three_below, three_above, *mates)
    )
    pairs = [
        pair, three_below, three_above,
        shift(jnp.concatenate([pair, three_above, three_below[:1]]), 1),
        shift(jnp.concatenate([pair, three_below, three_above[1:]]), -1),
    ]
    far = jnp.concatenate([far_low, far_high])
    below_across = lax.ppermute(across, "dp", X_UP)
    above_across = lax.ppermute(across, "dp", X_DOWN)
    far_across = lax.ppermute(far, "dp", Y_SWAP)
    far, below_across = lax.optimization_barrier((far, below_across))
    rest = [far, below_across, above_across, far_across]
    pieces = first + rest + mates + [lax.ppermute(piece, "dp", C_SWAP) for piece in rest]

    hidden, grads, ordered, *rows = dense_work(place, ranks, here, pieces, pairs, cotangent)
    send, keep = tile_work(target, ordered, grads)
    came = lax.ppermute(send, "dp", C_SWAP)

    def block(dx, dy, came=came):
        at = BLOCKS[dx, dy] * PER
        return keep[at:at + PER].astype(f32) + came[at:at + PER].astype(f32)

    sends = [block(*at).astype(bf16) for at in ((2, 1), (1, 1), (3, 1))]
    *sends, near_up, near_down = lax.optimization_barrier((*sends, rows[3], rows[4]))
    near_up, near_down = shift(near_up, 1), shift(near_down, -1)
    far_in = lax.ppermute(sends[0], "dp", Y_SWAP)
    up_in = lax.ppermute(sends[1], "dp", X_UP)
    down_in = lax.ppermute(sends[2], "dp", X_DOWN)
    far_in, up_in, down_in, near_up, near_down, late_one = lax.optimization_barrier(
        (far_in, up_in, down_in, near_up, near_down, came)
    )
    far_sum = block(2, 0, late_one) + far_in.astype(f32)
    across_sum = block(0, 1, late_one) + up_in.astype(f32) + down_in.astype(f32)
    sends = lax.optimization_barrier(
        (across_sum.astype(bf16), far_sum[:half].astype(bf16), far_sum[half:].astype(bf16))
    )
    gap = jnp.zeros_like(near_up[4:])
    three_up = rows[1].astype(f32) + near_down[2:4].astype(f32)
    three_up = three_up + jnp.concatenate([near_up[4:], gap]).astype(f32)
    three_down = rows[2].astype(f32) + near_up[2:4].astype(f32)
    three_down = three_down + jnp.concatenate([gap, near_down[4:]]).astype(f32)
    three_up, three_down = lax.optimization_barrier((three_up.astype(bf16), three_down.astype(bf16)))
    three_in_up, three_in_down = shift(three_up, 3), shift(three_down, -3)
    across_in = lax.ppermute(sends[0], "dp", Y_SWAP)
    half_up = lax.ppermute(sends[1], "dp", X_UP)
    half_down = lax.ppermute(sends[2], "dp", X_DOWN)
    half_up, half_down, late_two = lax.optimization_barrier((half_up, half_down, late_one))
    none = jnp.zeros_like(half_up)
    up_sum = block(1, 0, late_two) + jnp.concatenate([half_up, none]).astype(f32)
    down_sum = block(3, 0, late_two) + jnp.concatenate([none, half_down]).astype(f32)
    sends = lax.optimization_barrier((up_sum.astype(bf16), down_sum.astype(bf16)))
    up_last = lax.ppermute(sends[0], "dp", X_UP)
    down_last = lax.ppermute(sends[1], "dp", X_DOWN)
    up_last, down_last, across_in, late_three, three_in_up, three_in_down = lax.optimization_barrier(
        (up_last, down_last, across_in, late_two, three_in_up, three_in_down)
    )
    total = block(0, 0, late_three) + across_in.astype(f32)
    total = total + up_last.astype(f32) + down_last.astype(f32)
    tile_grads = (total * (1.0 / (XS * YS * CS)))[None]

    arrived = [rows[0], near_up[:2], near_down[:2], three_in_up, three_in_down]
    theirs = sum(part[1].astype(f32) for part in arrived).astype(bf16)
    back = lax.ppermute(theirs, "tensor", L_SWAP)
    grad_tokens = sum(part[0].astype(f32) for part in arrived) + back.astype(f32)
    grad_tokens = grad_tokens.astype(bf16)
    return hidden, grad_tokens, tile_grads


def solution(mesh):
    in_specs = (
        P(("dp", "tensor"), None),
        P("tensor", "dp", None, None, None),
        P(None, None, "tensor"),
        P("dp", "tensor"),
    )
    out_specs = (P("dp", "tensor"), P(("dp", "tensor"), None), P("tensor", "dp", None, None, None))
    return jax.shard_map(body, mesh=mesh, in_specs=in_specs, out_specs=out_specs, check_vma=False)
```

```python
import jax
import jax.numpy as jnp
from jax import lax
from jax.experimental import pallas as pl
from jax.experimental.pallas import tpu as pltpu
from jax.sharding import PartitionSpec as P

TILE = 128
ROWS = 32
COLS = 7
CAP = 128
PER = 8
GROUP = 256
WIDTH = ROWS * TILE
HIDE = COLS * TILE
DEAD = ROWS * COLS
XS, YS, CS = 4, 2, 2
ZS, YL = 8, 2


def dp_perm(move):
    def index(x, y, c):
        return (x * YS + y) * CS + c

    return [
        (index(x, y, c), index(*move(x, y, c)))
        for x in range(XS)
        for y in range(YS)
        for c in range(CS)
    ]


X_UP = dp_perm(lambda x, y, c: ((x + 1) % XS, y, c))
X_DOWN = dp_perm(lambda x, y, c: ((x - 1) % XS, y, c))
Y_SWAP = dp_perm(lambda x, y, c: (x, 1 - y, c))
C_SWAP = dp_perm(lambda x, y, c: (x, y, 1 - c))
L_SWAP = [(l * ZS + z, (1 - l) * ZS + z) for l in range(YL) for z in range(ZS)]
Z_RINGS = [[l * ZS + z for z in range(ZS)] for l in range(YL)]

BLOCKS = {(1, 1): 0, (3, 1): 1, (2, 1): 2, (0, 1): 3, (2, 0): 4, (1, 0): 5, (3, 0): 6, (0, 0): 7}
EARLY = 3 * PER
HALF = len(BLOCKS) * PER
PIECES = 2 * len(BLOCKS)
SPAN = 512
VMEM_LIMIT = 58 * 1024 * 1024


def start_rows(low, gathered, tokens, sems):
    copies = []
    for z in range(ZS):
        for l in range(YL):
            first = pl.multiple_of((low[0] ^ l) * (GROUP // YL) + z * 16, 16)
            copies.append(
                pltpu.make_async_copy(
                    gathered.at[z, l], tokens.at[pl.ds(first, 16)], sems.at[z * YL + l]
                )
            )
            copies[-1].start()
    return copies


def dense_kernel(*refs):
    place, ranks, low = refs[:3]
    pieces = refs[3:3 + PIECES]
    gathered, cotangent, hidden, grads, rows_out = refs[3 + PIECES:8 + PIECES]
    weight, stored, tokens, rows, piece_sems, row_sems, out_sems = refs[8 + PIECES:]
    copies = []
    for p in range(PIECES):
        copies.append(
            pltpu.make_async_copy(pieces[p], stored.at[pl.ds(p * PER, PER)], piece_sems.at[p])
        )
        copies[-1].start()
    row_copies = start_rows(low, gathered, tokens, row_sems)
    weight[...] = jnp.zeros_like(weight)
    for p in range(PIECES):
        copies[p].wait()
        for j in range(PER):
            for m in range(2):
                spot = place[m, ranks[p] * PER + j]
                weight[spot, :, m * TILE:(m + 1) * TILE] = stored[p * PER + j, m]
    for copy in row_copies:
        copy.wait()

    for c in range(COLS):
        dense = weight[c * ROWS:(c + 1) * ROWS].reshape(WIDTH, 2 * TILE)
        total = jnp.dot(tokens[...], dense, preferred_element_type=jnp.float32)
        gate, up = total[:, :TILE], total[:, TILE:]
        lanes = slice(c * TILE, (c + 1) * TILE)
        sigma = 1.0 / (1.0 + jnp.exp(-gate))
        swish = gate * sigma
        hidden[:, lanes] = (swish * up).astype(jnp.bfloat16)
        out_grad = cotangent[:, lanes].astype(jnp.float32)
        grads[c, :, TILE:] = (out_grad * swish).astype(jnp.bfloat16)
        grads[c, :, :TILE] = (
            out_grad * up * sigma * (1.0 + gate * (1.0 - sigma))
        ).astype(jnp.bfloat16)

    span = 256
    out_copies = []
    for part in range(WIDTH // span):
        total = jnp.zeros((GROUP, span), jnp.float32)
        for c in range(COLS):
            dense = weight[c * ROWS + part * 2:c * ROWS + part * 2 + 2].reshape(span, 2 * TILE)
            total += lax.dot_general(
                grads[c], dense, (((1,), (1,)), ((), ())), preferred_element_type=jnp.float32
            )
        lanes = slice(part * span, (part + 1) * span)
        for z in range(ZS):
            for l in range(YL):
                rows[z, l, :, lanes] = total[l * 128 + z * 16:l * 128 + z * 16 + 16]
        if part % 4 == 3:
            wide = pl.ds((part - 3) * span, 4 * span)
            out_copies.append(
                pltpu.make_async_copy(
                    rows.at[:, :, :, wide], rows_out.at[:, :, :, wide], out_sems.at[part // 4]
                )
            )
            out_copies[-1].start()
    for copy in out_copies:
        copy.wait()


def dense_work(place, ranks, low, pieces, gathered, cotangent):
    smem = pl.BlockSpec(memory_space=pltpu.SMEM)
    vmem = pl.BlockSpec(memory_space=pltpu.VMEM)
    hbm = pl.BlockSpec(memory_space=pl.ANY)
    bf16 = jnp.bfloat16
    return pl.pallas_call(
        dense_kernel,
        out_shape=(
            jax.ShapeDtypeStruct((GROUP, HIDE), bf16),
            jax.ShapeDtypeStruct((COLS, GROUP, 2 * TILE), bf16),
            jax.ShapeDtypeStruct((ZS, YL, 16, WIDTH), jnp.float32),
        ),
        in_specs=[smem] * 3 + [hbm] * (PIECES + 1) + [vmem],
        out_specs=(vmem, vmem, hbm),
        scratch_shapes=[
            pltpu.VMEM((DEAD + 1, TILE, 2 * TILE), bf16),
            pltpu.VMEM((CAP, 2, TILE, TILE), bf16),
            pltpu.VMEM((GROUP, WIDTH), bf16),
            pltpu.VMEM((ZS, YL, 16, WIDTH), jnp.float32),
            pltpu.SemaphoreType.DMA((PIECES,)),
            pltpu.SemaphoreType.DMA((ZS * YL,)),
            pltpu.SemaphoreType.DMA((4,)),
        ],
        compiler_params=pltpu.CompilerParams(vmem_limit_bytes=VMEM_LIMIT),
        cost_estimate=pl.CostEstimate(
            flops=4 * GROUP * WIDTH * 2 * HIDE, bytes_accessed=16 << 20, transcendentals=GROUP * HIDE
        ),
        name="forward_and_rows",
    )(place, ranks, low, *pieces, gathered, cotangent)


def tile_kernel(
    target, ready, spots, low, gathered, grads, early_out, late_out, keep_out,
    tokens, turned, tiles, row_sems, sems,
):
    row_copies = start_rows(low, gathered, tokens, row_sems)
    tiles[...] = jnp.zeros_like(tiles)
    for copy in row_copies:
        copy.wait()
    for r in range(0, WIDTH, 512):
        turned[r:r + 512, :] = tokens[:, r:r + 512].T
    outs = [(early_out, 0, EARLY), (late_out, EARLY, HALF - EARLY), (keep_out, HALF, HALF)]

    def send_block(k, unused):
        spot = pl.multiple_of(spots[k], PER)
        for i, (out, first, count) in enumerate(outs):
            @pl.when((spot >= first) & (spot < first + count))
            def _():
                pltpu.make_async_copy(
                    tiles.at[pl.ds(spot, PER)], out.at[pl.ds(spot - first, PER)], sems.at[i]
                ).start()
        return unused

    def chunk(part, done):
        rows = pl.ds(pl.multiple_of(part * SPAN, SPAN), SPAN)
        for c in range(COLS):
            total = jnp.dot(
                turned[rows, :], grads[c], preferred_element_type=jnp.float32
            ).astype(jnp.bfloat16)
            for i in range(SPAN // TILE):
                for m in range(2):
                    spot = target[m, (part * (SPAN // TILE) + i) * COLS + c]
                    tiles[spot, m] = total[i * TILE:(i + 1) * TILE, m * TILE:(m + 1) * TILE]
        lax.fori_loop(done, ready[part], send_block, 0)
        return ready[part]

    lax.fori_loop(0, WIDTH // SPAN, chunk, 0)
    for i, (out, first, count) in enumerate(outs):
        pltpu.make_async_copy(tiles.at[pl.ds(first, count)], out, sems.at[i]).wait()


def tile_work(target, ready, spots, low, gathered, grads):
    smem = pl.BlockSpec(memory_space=pltpu.SMEM)
    vmem = pl.BlockSpec(memory_space=pltpu.VMEM)
    hbm = pl.BlockSpec(memory_space=pl.ANY)
    bf16 = jnp.bfloat16
    return pl.pallas_call(
        tile_kernel,
        out_shape=tuple(
            jax.ShapeDtypeStruct((n, 2, TILE, TILE), bf16) for n in (EARLY, HALF - EARLY, HALF)
        ),
        in_specs=[smem] * 4 + [hbm, vmem],
        out_specs=(hbm,) * 3,
        scratch_shapes=[
            pltpu.VMEM((GROUP, WIDTH), bf16),
            pltpu.VMEM((WIDTH, GROUP), bf16),
            pltpu.VMEM((CAP + 1, 2, TILE, TILE), bf16),
            pltpu.SemaphoreType.DMA((ZS * YL,)),
            pltpu.SemaphoreType.DMA((3,)),
        ],
        compiler_params=pltpu.CompilerParams(vmem_limit_bytes=VMEM_LIMIT),
        cost_estimate=pl.CostEstimate(
            flops=2 * GROUP * WIDTH * 2 * HIDE, bytes_accessed=12 << 20, transcendentals=0
        ),
        name="tile_sums",
    )(target, ready, spots, low, gathered, grads)


def tables(keep_local, x, y, c):
    keep = keep_local.reshape(2, ROWS * COLS)
    places = jnp.arange(ROWS * COLS, dtype=jnp.int32)
    order = jnp.sum(jnp.where(places[None, :] <= places[:, None], keep[:, None, :], 0), axis=2) - 1
    dense_spot = (places % COLS) * ROWS + places // COLS
    slots = jnp.arange(CAP, dtype=jnp.int32)
    match = (order[:, None, :] == slots[None, :, None]) & (keep[:, None, :] == 1)
    place = DEAD + jnp.sum(jnp.where(match, dense_spot - DEAD, 0), axis=2)

    def spot_of(owner):
        dx = ((owner >> 2) - x) & (XS - 1)
        dy = ((owner >> 1) & 1) ^ y
        dc = (owner & 1) ^ c
        block = jnp.zeros_like(owner)
        for (a, b), at in BLOCKS.items():
            block = jnp.where((dx == a) & (dy == b), at, block)
        return ((1 - dc) * len(BLOCKS) + block) * PER

    target = jnp.where(keep == 1, spot_of(order >> 3) + (order & (PER - 1)), CAP)
    spots = spot_of(jnp.arange(XS * YS * CS, dtype=jnp.int32))
    chunks = jnp.arange(1, WIDTH // SPAN + 1, dtype=jnp.int32)
    inside = places[None, :] < (chunks * (SPAN // TILE * COLS))[:, None]
    counts = jnp.sum(jnp.where(inside[None], keep[:, None, :], 0), axis=2)
    ready = jnp.where(chunks == WIDTH // SPAN, XS * YS * CS, jnp.min(counts, axis=0) >> 3)
    return place.astype(jnp.int32), target.astype(jnp.int32), ready.astype(jnp.int32), spots


def piece_ranks(x, y, c):
    spots = [(0, 0), (3, 0), (1, 0), (0, 1), (2, 0), (3, 1), (1, 1), (2, 1)]
    dx = jnp.array([a for a, b in spots] * 2, jnp.int32)
    dy = jnp.array([b for a, b in spots] * 2, jnp.int32)
    dc = jnp.array([0] * len(spots) + [1] * len(spots), jnp.int32)
    return (((x + dx) & (XS - 1)) * YS + (y ^ dy)) * CS + (c ^ dc)


def join_kernel(low, high, out):
    out[:PER // 2] = low[...]
    out[PER // 2:] = high[...]


def join(low, high):
    return pl.pallas_call(
        join_kernel,
        out_shape=jax.ShapeDtypeStruct((PER, 2, TILE, TILE), low.dtype),
        in_specs=[pl.BlockSpec(memory_space=pltpu.VMEM)] * 2,
        out_specs=pl.BlockSpec(memory_space=pltpu.VMEM),
        cost_estimate=pl.CostEstimate(flops=20000000000, bytes_accessed=2 << 20, transcendentals=0),
        name="join_halves",
    )(low, high)


def body(tokens, weight_tiles, keep_mask, cotangent):
    f32, bf16 = jnp.float32, jnp.bfloat16
    rank = lax.axis_index("dp")
    x, y, c = rank >> 2, (rank >> 1) & 1, rank & 1
    low = lax.axis_index("tensor") >> 3

    other = lax.ppermute(tokens, "tensor", L_SWAP)
    own = weight_tiles[0]
    below = lax.ppermute(own, "dp", X_UP)
    above = lax.ppermute(own, "dp", X_DOWN)
    across = lax.ppermute(own, "dp", Y_SWAP)
    pair = jnp.stack([tokens, other])
    gathered = lax.all_gather(pair, "tensor", axis=0, axis_index_groups=Z_RINGS)
    place, target, ready, spots = lax.optimization_barrier(tables(keep_mask, x, y, c))
    ranks = piece_ranks(x, y, c)
    half = PER // 2
    far_low = lax.ppermute(below[:half], "dp", X_UP)
    far_high = lax.ppermute(above[half:], "dp", X_DOWN)
    far = join(far_low, far_high)
    below_across = lax.ppermute(across, "dp", X_UP)
    above_across = lax.ppermute(across, "dp", X_DOWN)
    far_across = lax.ppermute(far, "dp", Y_SWAP)
    pieces = [own, below, above, across, far, below_across, above_across, far_across]
    pieces = pieces + [lax.ppermute(piece, "dp", C_SWAP) for piece in pieces]
    low_table = low.reshape(1).astype(jnp.int32)

    hidden, grads, rows = dense_work(place, ranks, low_table, pieces, gathered, cotangent)
    summed = lax.psum_scatter(rows, "tensor", scatter_dimension=0, axis_index_groups=Z_RINGS)
    early, late, keep = tile_work(target, ready, spots, low_table, gathered, grads)

    early_in = lax.ppermute(early, "dp", C_SWAP)

    def block(dx, dy, late_in=None):
        at = BLOCKS[dx, dy] * PER
        came = early_in[at:at + PER] if at < EARLY else late_in[at - EARLY:at - EARLY + PER]
        return keep[at:at + PER].astype(f32) + came.astype(f32)

    sends = [block(*at).astype(bf16) for at in ((2, 1), (1, 1), (3, 1))]
    *sends, late = lax.optimization_barrier((*sends, late))
    far_in = lax.ppermute(sends[0], "dp", Y_SWAP)
    up_in = lax.ppermute(sends[1], "dp", X_UP)
    down_in = lax.ppermute(sends[2], "dp", X_DOWN)
    late_in = lax.ppermute(late, "dp", C_SWAP)
    far_in, up_in, down_in, late_one = lax.optimization_barrier((far_in, up_in, down_in, late_in))
    far_sum = block(2, 0, late_one) + far_in.astype(f32)
    across_sum = block(0, 1, late_one) + up_in.astype(f32) + down_in.astype(f32)
    sends = lax.optimization_barrier(
        (across_sum.astype(bf16), far_sum[:half].astype(bf16), far_sum[half:].astype(bf16))
    )
    across_in = lax.ppermute(sends[0], "dp", Y_SWAP)
    half_up = lax.ppermute(sends[1], "dp", X_UP)
    half_down = lax.ppermute(sends[2], "dp", X_DOWN)
    half_up, half_down, late_two = lax.optimization_barrier((half_up, half_down, late_one))
    none = jnp.zeros_like(half_up)
    up_sum = block(1, 0, late_two) + jnp.concatenate([half_up, none]).astype(f32)
    down_sum = block(3, 0, late_two) + jnp.concatenate([none, half_down]).astype(f32)
    sends = lax.optimization_barrier((up_sum.astype(bf16), down_sum.astype(bf16)))
    up_last = lax.ppermute(sends[0], "dp", X_UP)
    down_last = lax.ppermute(sends[1], "dp", X_DOWN)
    up_last, down_last, across_in, late_three = lax.optimization_barrier(
        (up_last, down_last, across_in, late_two)
    )
    total = block(0, 0, late_three) + across_in.astype(f32)
    total = total + up_last.astype(f32) + down_last.astype(f32)
    tile_grads = (total * (1.0 / (XS * YS * CS)))[None]

    mine = jnp.where(low == 0, summed[0], summed[1])
    theirs = jnp.where(low == 0, summed[1], summed[0])
    back = lax.ppermute(theirs.astype(bf16), "tensor", L_SWAP)
    grad_tokens = (mine + back.astype(f32)).astype(bf16)
    return hidden, grad_tokens, tile_grads


def solution(mesh):
    in_specs = (
        P(("dp", "tensor"), None),
        P("tensor", "dp", None, None, None),
        P(None, None, "tensor"),
        P("dp", "tensor"),
    )
    out_specs = (P("dp", "tensor"), P(("dp", "tensor"), None), P("tensor", "dp", None, None, None))
    return jax.shard_map(body, mesh=mesh, in_specs=in_specs, out_specs=out_specs, check_vma=False)
```

```python
import jax
import jax.numpy as jnp
from jax import lax
from jax.experimental import pallas as pl
from jax.experimental.pallas import tpu as pltpu
from jax.sharding import PartitionSpec as P

TILE = 128
ROWS = 32
COLS = 7
CAP = 128
PER = 8
GROUP = 256
WIDTH = ROWS * TILE
HIDE = COLS * TILE
DEAD = ROWS * COLS
XS, YS, CS = 4, 2, 2
ZS, YL = 8, 2


def dp_perm(move):
    def index(x, y, c):
        return (x * YS + y) * CS + c

    return [
        (index(x, y, c), index(*move(x, y, c)))
        for x in range(XS)
        for y in range(YS)
        for c in range(CS)
    ]


X_UP = dp_perm(lambda x, y, c: ((x + 1) % XS, y, c))
X_DOWN = dp_perm(lambda x, y, c: ((x - 1) % XS, y, c))
Y_SWAP = dp_perm(lambda x, y, c: (x, 1 - y, c))
C_SWAP = dp_perm(lambda x, y, c: (x, y, 1 - c))
L_SWAP = [(l * ZS + z, (1 - l) * ZS + z) for l in range(YL) for z in range(ZS)]
Z_RINGS = [[l * ZS + z for z in range(ZS)] for l in range(YL)]

BLOCKS = {(1, 1): 0, (3, 1): 1, (2, 1): 2, (0, 1): 3, (2, 0): 4, (1, 0): 5, (3, 0): 6, (0, 0): 7}
EARLY = 3 * PER
HALF = len(BLOCKS) * PER
PIECES = 2 * len(BLOCKS)
SPAN = 512
DENSE_LIMIT = 58 * 1024 * 1024
TILE_LIMIT = 20 * 1024 * 1024


def start_rows(low, gathered, tokens, sems):
    copies = []
    for z in range(ZS):
        for l in range(YL):
            first = pl.multiple_of((low[0] ^ l) * (GROUP // YL) + z * 16, 16)
            copies.append(
                pltpu.make_async_copy(
                    gathered.at[z, l], tokens.at[pl.ds(first, 16)], sems.at[z * YL + l]
                )
            )
            copies[-1].start()
    return copies


def dense_kernel(*refs):
    place, ranks, low = refs[:3]
    pieces = refs[3:3 + PIECES]
    gathered, cotangent, hidden, grads, rows_out = refs[3 + PIECES:8 + PIECES]
    weight, stored, tokens, rows, piece_sems, row_sems, out_sems = refs[8 + PIECES:]
    copies = []
    for p in range(PIECES):
        copies.append(
            pltpu.make_async_copy(pieces[p], stored.at[pl.ds(p * PER, PER)], piece_sems.at[p])
        )
        copies[-1].start()
    row_copies = start_rows(low, gathered, tokens, row_sems)
    weight[...] = jnp.zeros_like(weight)
    for p in range(PIECES):
        copies[p].wait()
        for j in range(PER):
            for m in range(2):
                spot = place[m, ranks[p] * PER + j]
                weight[spot, :, m * TILE:(m + 1) * TILE] = stored[p * PER + j, m]
    for copy in row_copies:
        copy.wait()

    for c in range(COLS):
        dense = weight[c * ROWS:(c + 1) * ROWS].reshape(WIDTH, 2 * TILE)
        total = jnp.dot(tokens[...], dense, preferred_element_type=jnp.float32)
        gate, up = total[:, :TILE], total[:, TILE:]
        lanes = slice(c * TILE, (c + 1) * TILE)
        sigma = 1.0 / (1.0 + jnp.exp(-gate))
        swish = gate * sigma
        hidden[:, lanes] = (swish * up).astype(jnp.bfloat16)
        out_grad = cotangent[:, lanes].astype(jnp.float32)
        grads[c, :, TILE:] = (out_grad * swish).astype(jnp.bfloat16)
        grads[c, :, :TILE] = (
            out_grad * up * sigma * (1.0 + gate * (1.0 - sigma))
        ).astype(jnp.bfloat16)

    span = 256
    out_copies = []
    for part in range(WIDTH // span):
        total = jnp.zeros((GROUP, span), jnp.float32)
        for c in range(COLS):
            dense = weight[c * ROWS + part * 2:c * ROWS + part * 2 + 2].reshape(span, 2 * TILE)
            total += lax.dot_general(
                grads[c], dense, (((1,), (1,)), ((), ())), preferred_element_type=jnp.float32
            )
        lanes = slice(part * span, (part + 1) * span)
        for z in range(ZS):
            for l in range(YL):
                rows[z, l, :, lanes] = total[l * 128 + z * 16:l * 128 + z * 16 + 16]
        if part % 4 == 3:
            wide = pl.ds((part - 3) * span, 4 * span)
            out_copies.append(
                pltpu.make_async_copy(
                    rows.at[:, :, :, wide], rows_out.at[:, :, :, wide], out_sems.at[part // 4]
                )
            )
            out_copies[-1].start()
    for copy in out_copies:
        copy.wait()


def dense_work(place, ranks, low, pieces, gathered, cotangent):
    smem = pl.BlockSpec(memory_space=pltpu.SMEM)
    vmem = pl.BlockSpec(memory_space=pltpu.VMEM)
    hbm = pl.BlockSpec(memory_space=pl.ANY)
    bf16 = jnp.bfloat16
    return pl.pallas_call(
        dense_kernel,
        out_shape=(
            jax.ShapeDtypeStruct((GROUP, HIDE), bf16),
            jax.ShapeDtypeStruct((COLS, GROUP, 2 * TILE), bf16),
            jax.ShapeDtypeStruct((ZS, YL, 16, WIDTH), jnp.float32),
        ),
        in_specs=[smem] * 3 + [hbm] * (PIECES + 1) + [vmem],
        out_specs=(vmem, vmem, hbm),
        scratch_shapes=[
            pltpu.VMEM((DEAD + 1, TILE, 2 * TILE), bf16),
            pltpu.VMEM((CAP, 2, TILE, TILE), bf16),
            pltpu.VMEM((GROUP, WIDTH), bf16),
            pltpu.VMEM((ZS, YL, 16, WIDTH), jnp.float32),
            pltpu.SemaphoreType.DMA((PIECES,)),
            pltpu.SemaphoreType.DMA((ZS * YL,)),
            pltpu.SemaphoreType.DMA((4,)),
        ],
        compiler_params=pltpu.CompilerParams(vmem_limit_bytes=DENSE_LIMIT),
        cost_estimate=pl.CostEstimate(
            flops=4 * GROUP * WIDTH * 2 * HIDE, bytes_accessed=16 << 20, transcendentals=GROUP * HIDE
        ),
        name="forward_and_rows",
    )(place, ranks, low, *pieces, gathered, cotangent)


def tile_kernel(
    target, ready, spots, low, gathered, grads, early_out, late_out, keep_out,
    tokens, turned, tiles, row_sems, sems,
):
    row_copies = start_rows(low, gathered, tokens, row_sems)
    tiles[...] = jnp.zeros_like(tiles)
    for copy in row_copies:
        copy.wait()
    for r in range(0, WIDTH, 512):
        turned[r:r + 512, :] = tokens[:, r:r + 512].T
    outs = [(early_out, 0, EARLY), (late_out, EARLY, HALF - EARLY), (keep_out, HALF, HALF)]

    def send_block(k, unused):
        spot = pl.multiple_of(spots[k], PER)
        for i, (out, first, count) in enumerate(outs):
            @pl.when((spot >= first) & (spot < first + count))
            def _():
                pltpu.make_async_copy(
                    tiles.at[pl.ds(spot, PER)], out.at[pl.ds(spot - first, PER)], sems.at[i]
                ).start()
        return unused

    def chunk(part, done):
        rows = pl.ds(pl.multiple_of(part * SPAN, SPAN), SPAN)
        for c in range(COLS):
            total = jnp.dot(
                turned[rows, :], grads[c], preferred_element_type=jnp.float32
            ).astype(jnp.bfloat16)
            for i in range(SPAN // TILE):
                for m in range(2):
                    spot = target[m, (part * (SPAN // TILE) + i) * COLS + c]
                    tiles[spot, m] = total[i * TILE:(i + 1) * TILE, m * TILE:(m + 1) * TILE]
        lax.fori_loop(done, ready[part], send_block, 0)
        return ready[part]

    lax.fori_loop(0, WIDTH // SPAN, chunk, 0)
    for i, (out, first, count) in enumerate(outs):
        pltpu.make_async_copy(tiles.at[pl.ds(first, count)], out, sems.at[i]).wait()


def tile_work(target, ready, spots, low, gathered, grads):
    smem = pl.BlockSpec(memory_space=pltpu.SMEM)
    vmem = pl.BlockSpec(memory_space=pltpu.VMEM)
    hbm = pl.BlockSpec(memory_space=pl.ANY)
    bf16 = jnp.bfloat16
    return pl.pallas_call(
        tile_kernel,
        out_shape=tuple(
            jax.ShapeDtypeStruct((n, 2, TILE, TILE), bf16) for n in (EARLY, HALF - EARLY, HALF)
        ),
        in_specs=[smem] * 4 + [hbm, vmem],
        out_specs=(hbm,) * 3,
        scratch_shapes=[
            pltpu.VMEM((GROUP, WIDTH), bf16),
            pltpu.VMEM((WIDTH, GROUP), bf16),
            pltpu.VMEM((CAP + 1, 2, TILE, TILE), bf16),
            pltpu.SemaphoreType.DMA((ZS * YL,)),
            pltpu.SemaphoreType.DMA((3,)),
        ],
        compiler_params=pltpu.CompilerParams(vmem_limit_bytes=TILE_LIMIT),
        cost_estimate=pl.CostEstimate(
            flops=2 * GROUP * WIDTH * 2 * HIDE, bytes_accessed=12 << 20, transcendentals=0
        ),
        name="tile_sums",
    )(target, ready, spots, low, gathered, grads)


def tables(keep_local, x, y, c):
    keep = keep_local.reshape(2, ROWS * COLS)
    places = jnp.arange(ROWS * COLS, dtype=jnp.int32)
    order = jnp.sum(jnp.where(places[None, :] <= places[:, None], keep[:, None, :], 0), axis=2) - 1
    dense_spot = (places % COLS) * ROWS + places // COLS
    slots = jnp.arange(CAP, dtype=jnp.int32)
    match = (order[:, None, :] == slots[None, :, None]) & (keep[:, None, :] == 1)
    place = DEAD + jnp.sum(jnp.where(match, dense_spot - DEAD, 0), axis=2)

    def spot_of(owner):
        dx = ((owner >> 2) - x) & (XS - 1)
        dy = ((owner >> 1) & 1) ^ y
        dc = (owner & 1) ^ c
        block = jnp.zeros_like(owner)
        for (a, b), at in BLOCKS.items():
            block = jnp.where((dx == a) & (dy == b), at, block)
        return ((1 - dc) * len(BLOCKS) + block) * PER

    target = jnp.where(keep == 1, spot_of(order >> 3) + (order & (PER - 1)), CAP)
    spots = spot_of(jnp.arange(XS * YS * CS, dtype=jnp.int32))
    chunks = jnp.arange(1, WIDTH // SPAN + 1, dtype=jnp.int32)
    inside = places[None, :] < (chunks * (SPAN // TILE * COLS))[:, None]
    counts = jnp.sum(jnp.where(inside[None], keep[:, None, :], 0), axis=2)
    ready = jnp.where(chunks == WIDTH // SPAN, XS * YS * CS, jnp.min(counts, axis=0) >> 3)
    return place.astype(jnp.int32), target.astype(jnp.int32), ready.astype(jnp.int32), spots


def piece_ranks(x, y, c):
    spots = [(0, 0), (3, 0), (1, 0), (0, 1), (2, 0), (3, 1), (1, 1), (2, 1)]
    dx = jnp.array([a for a, b in spots] * 2, jnp.int32)
    dy = jnp.array([b for a, b in spots] * 2, jnp.int32)
    dc = jnp.array([0] * len(spots) + [1] * len(spots), jnp.int32)
    return (((x + dx) & (XS - 1)) * YS + (y ^ dy)) * CS + (c ^ dc)


def join_kernel(low, high, out):
    out[:PER // 2] = low[...]
    out[PER // 2:] = high[...]


def join(low, high):
    return pl.pallas_call(
        join_kernel,
        out_shape=jax.ShapeDtypeStruct((PER, 2, TILE, TILE), low.dtype),
        in_specs=[pl.BlockSpec(memory_space=pltpu.VMEM)] * 2,
        out_specs=pl.BlockSpec(memory_space=pltpu.VMEM),
        cost_estimate=pl.CostEstimate(flops=20000000000, bytes_accessed=2 << 20, transcendentals=0),
        name="join_halves",
    )(low, high)


def body(tokens, weight_tiles, keep_mask, cotangent):
    f32, bf16 = jnp.float32, jnp.bfloat16
    rank = lax.axis_index("dp")
    x, y, c = rank >> 2, (rank >> 1) & 1, rank & 1
    low = lax.axis_index("tensor") >> 3

    other = lax.ppermute(tokens, "tensor", L_SWAP)
    own = weight_tiles[0]
    below = lax.ppermute(own, "dp", X_UP)
    above = lax.ppermute(own, "dp", X_DOWN)
    across = lax.ppermute(own, "dp", Y_SWAP)
    pair = jnp.stack([tokens, other])
    gathered = lax.all_gather(pair, "tensor", axis=0, axis_index_groups=Z_RINGS)
    place, target, ready, spots = lax.optimization_barrier(tables(keep_mask, x, y, c))
    ranks = piece_ranks(x, y, c)
    half = PER // 2
    far_low = lax.ppermute(below[:half], "dp", X_UP)
    far_high = lax.ppermute(above[half:], "dp", X_DOWN)
    far = join(far_low, far_high)
    below_across = lax.ppermute(across, "dp", X_UP)
    above_across = lax.ppermute(across, "dp", X_DOWN)
    far_across = lax.ppermute(far, "dp", Y_SWAP)
    pieces = [own, below, above, across, far, below_across, above_across, far_across]
    pieces = pieces + [lax.ppermute(piece, "dp", C_SWAP) for piece in pieces]
    low_table = low.reshape(1).astype(jnp.int32)

    hidden, grads, rows = dense_work(place, ranks, low_table, pieces, gathered, cotangent)
    summed = lax.psum_scatter(rows, "tensor", scatter_dimension=0, axis_index_groups=Z_RINGS)
    early, late, keep = tile_work(target, ready, spots, low_table, gathered, grads)

    early_in = lax.ppermute(early, "dp", C_SWAP)

    def block(dx, dy, late_in=None):
        at = BLOCKS[dx, dy] * PER
        came = early_in[at:at + PER] if at < EARLY else late_in[at - EARLY:at - EARLY + PER]
        return keep[at:at + PER].astype(f32) + came.astype(f32)

    sends = [block(*at).astype(bf16) for at in ((2, 1), (1, 1), (3, 1))]
    *sends, late = lax.optimization_barrier((*sends, late))
    far_in = lax.ppermute(sends[0], "dp", Y_SWAP)
    up_in = lax.ppermute(sends[1], "dp", X_UP)
    down_in = lax.ppermute(sends[2], "dp", X_DOWN)
    late_in = lax.ppermute(late, "dp", C_SWAP)
    far_in, up_in, down_in, late_one = lax.optimization_barrier((far_in, up_in, down_in, late_in))
    far_sum = block(2, 0, late_one) + far_in.astype(f32)
    across_sum = block(0, 1, late_one) + up_in.astype(f32) + down_in.astype(f32)
    sends = lax.optimization_barrier(
        (across_sum.astype(bf16), far_sum[:half].astype(bf16), far_sum[half:].astype(bf16))
    )
    across_in = lax.ppermute(sends[0], "dp", Y_SWAP)
    half_up = lax.ppermute(sends[1], "dp", X_UP)
    half_down = lax.ppermute(sends[2], "dp", X_DOWN)
    half_up, half_down, late_two = lax.optimization_barrier((half_up, half_down, late_one))
    none = jnp.zeros_like(half_up)
    up_sum = block(1, 0, late_two) + jnp.concatenate([half_up, none]).astype(f32)
    down_sum = block(3, 0, late_two) + jnp.concatenate([none, half_down]).astype(f32)
    sends = lax.optimization_barrier((up_sum.astype(bf16), down_sum.astype(bf16)))
    up_last = lax.ppermute(sends[0], "dp", X_UP)
    down_last = lax.ppermute(sends[1], "dp", X_DOWN)
    up_last, down_last, across_in, late_three = lax.optimization_barrier(
        (up_last, down_last, across_in, late_two)
    )
    total = block(0, 0, late_three) + across_in.astype(f32)
    total = total + up_last.astype(f32) + down_last.astype(f32)
    tile_grads = (total * (1.0 / (XS * YS * CS)))[None]

    mine = jnp.where(low == 0, summed[0], summed[1])
    theirs = jnp.where(low == 0, summed[1], summed[0])
    back = lax.ppermute(theirs.astype(bf16), "tensor", L_SWAP)
    grad_tokens = (mine + back.astype(f32)).astype(bf16)
    return hidden, grad_tokens, tile_grads


def solution(mesh):
    in_specs = (
        P(("dp", "tensor"), None),
        P("tensor", "dp", None, None, None),
        P(None, None, "tensor"),
        P("dp", "tensor"),
    )
    out_specs = (P("dp", "tensor"), P(("dp", "tensor"), None), P("tensor", "dp", None, None, None))
    return jax.shard_map(body, mesh=mesh, in_specs=in_specs, out_specs=out_specs, check_vma=False)
```

```python
import jax
import jax.numpy as jnp
from jax import lax
from jax.experimental import pallas as pl
from jax.experimental.pallas import tpu as pltpu
from jax.sharding import PartitionSpec as P

TILE = 128
ROWS = 32
COLS = 7
CAP = 128
PER = 8
GROUP = 256
WIDTH = ROWS * TILE
HIDE = COLS * TILE
DEAD = ROWS * COLS
XS, YS, CS = 4, 2, 2
ZS, YL = 8, 2


def dp_perm(move):
    def index(x, y, c):
        return (x * YS + y) * CS + c

    return [
        (index(x, y, c), index(*move(x, y, c)))
        for x in range(XS)
        for y in range(YS)
        for c in range(CS)
    ]


X_UP = dp_perm(lambda x, y, c: ((x + 1) % XS, y, c))
X_DOWN = dp_perm(lambda x, y, c: ((x - 1) % XS, y, c))
Y_SWAP = dp_perm(lambda x, y, c: (x, 1 - y, c))
C_SWAP = dp_perm(lambda x, y, c: (x, y, 1 - c))
L_SWAP = [(l * ZS + z, (1 - l) * ZS + z) for l in range(YL) for z in range(ZS)]
Z_RINGS = [[l * ZS + z for z in range(ZS)] for l in range(YL)]

BLOCKS = {(1, 1): 0, (3, 1): 1, (2, 1): 2, (0, 1): 3, (2, 0): 4, (1, 0): 5, (3, 0): 6, (0, 0): 7}
EARLY = 3 * PER
HALF = len(BLOCKS) * PER
PIECES = 2 * len(BLOCKS)
SPAN = 512
VMEM_LIMIT = 58 * 1024 * 1024


def start_rows(low, gathered, tokens, sems):
    copies = []
    for z in range(ZS):
        for l in range(YL):
            first = pl.multiple_of((low[0] ^ l) * (GROUP // YL) + z * 16, 16)
            copies.append(
                pltpu.make_async_copy(
                    gathered.at[z, l], tokens.at[pl.ds(first, 16)], sems.at[z * YL + l]
                )
            )
            copies[-1].start()
    return copies


def dense_kernel(*refs):
    place, ranks, low = refs[:3]
    pieces = refs[3:3 + PIECES]
    gathered, cotangent, hidden, grads, rows_out = refs[3 + PIECES:8 + PIECES]
    weight, stored, tokens, rows, piece_sems, row_sems, out_sems = refs[8 + PIECES:]
    copies = []
    for p in range(PIECES):
        copies.append(
            pltpu.make_async_copy(pieces[p], stored.at[pl.ds(p * PER, PER)], piece_sems.at[p])
        )
        copies[-1].start()
    row_copies = start_rows(low, gathered, tokens, row_sems)
    weight[...] = jnp.zeros_like(weight)
    for p in range(PIECES):
        copies[p].wait()
        for j in range(PER):
            for m in range(2):
                spot = place[m, ranks[p] * PER + j]
                weight[spot, :, m * TILE:(m + 1) * TILE] = stored[p * PER + j, m]
    for copy in row_copies:
        copy.wait()

    for c in range(COLS):
        dense = weight[c * ROWS:(c + 1) * ROWS].reshape(WIDTH, 2 * TILE)
        total = jnp.dot(tokens[...], dense, preferred_element_type=jnp.float32)
        gate, up = total[:, :TILE], total[:, TILE:]
        lanes = slice(c * TILE, (c + 1) * TILE)
        sigma = 1.0 / (1.0 + jnp.exp(-gate))
        swish = gate * sigma
        hidden[:, lanes] = (swish * up).astype(jnp.bfloat16)
        out_grad = cotangent[:, lanes].astype(jnp.float32)
        grads[c, :, TILE:] = (out_grad * swish).astype(jnp.bfloat16)
        grads[c, :, :TILE] = (
            out_grad * up * sigma * (1.0 + gate * (1.0 - sigma))
        ).astype(jnp.bfloat16)

    span = 256
    out_copies = []
    for part in range(WIDTH // span):
        total = jnp.zeros((GROUP, span), jnp.float32)
        for c in range(COLS):
            dense = weight[c * ROWS + part * 2:c * ROWS + part * 2 + 2].reshape(span, 2 * TILE)
            total += lax.dot_general(
                grads[c], dense, (((1,), (1,)), ((), ())), preferred_element_type=jnp.float32
            )
        lanes = slice(part * span, (part + 1) * span)
        for z in range(ZS):
            for l in range(YL):
                rows[z, l, :, lanes] = total[l * 128 + z * 16:l * 128 + z * 16 + 16]
        if part % 4 == 3:
            wide = pl.ds((part - 3) * span, 4 * span)
            out_copies.append(
                pltpu.make_async_copy(
                    rows.at[:, :, :, wide], rows_out.at[:, :, :, wide], out_sems.at[part // 4]
                )
            )
            out_copies[-1].start()
    for copy in out_copies:
        copy.wait()


def dense_work(place, ranks, low, pieces, gathered, cotangent):
    smem = pl.BlockSpec(memory_space=pltpu.SMEM)
    vmem = pl.BlockSpec(memory_space=pltpu.VMEM)
    hbm = pl.BlockSpec(memory_space=pl.ANY)
    bf16 = jnp.bfloat16
    return pl.pallas_call(
        dense_kernel,
        out_shape=(
            jax.ShapeDtypeStruct((GROUP, HIDE), bf16),
            jax.ShapeDtypeStruct((COLS, GROUP, 2 * TILE), bf16),
            jax.ShapeDtypeStruct((ZS, YL, 16, WIDTH), jnp.float32),
        ),
        in_specs=[smem] * 3 + [hbm] * (PIECES + 1) + [vmem],
        out_specs=(vmem, vmem, hbm),
        scratch_shapes=[
            pltpu.VMEM((DEAD + 1, TILE, 2 * TILE), bf16),
            pltpu.VMEM((CAP, 2, TILE, TILE), bf16),
            pltpu.VMEM((GROUP, WIDTH), bf16),
            pltpu.VMEM((ZS, YL, 16, WIDTH), jnp.float32),
            pltpu.SemaphoreType.DMA((PIECES,)),
            pltpu.SemaphoreType.DMA((ZS * YL,)),
            pltpu.SemaphoreType.DMA((4,)),
        ],
        compiler_params=pltpu.CompilerParams(vmem_limit_bytes=VMEM_LIMIT),
        cost_estimate=pl.CostEstimate(
            flops=4 * GROUP * WIDTH * 2 * HIDE, bytes_accessed=16 << 20, transcendentals=GROUP * HIDE
        ),
        name="forward_and_rows",
    )(place, ranks, low, *pieces, gathered, cotangent)


def tile_kernel(
    target, ready, spots, low, gathered, grads, early_out, late_out, keep_out,
    tokens, turned, tiles, row_sems, sems,
):
    row_copies = start_rows(low, gathered, tokens, row_sems)
    tiles[...] = jnp.zeros_like(tiles)
    for copy in row_copies:
        copy.wait()
    for r in range(0, WIDTH, 512):
        turned[r:r + 512, :] = tokens[:, r:r + 512].T
    outs = [(early_out, 0, EARLY), (late_out, EARLY, HALF - EARLY), (keep_out, HALF, HALF)]

    def send_block(k, unused):
        spot = pl.multiple_of(spots[k], PER)
        for i, (out, first, count) in enumerate(outs):
            @pl.when((spot >= first) & (spot < first + count))
            def _():
                pltpu.make_async_copy(
                    tiles.at[pl.ds(spot, PER)], out.at[pl.ds(spot - first, PER)], sems.at[i]
                ).start()
        return unused

    def chunk(part, done):
        rows = pl.ds(pl.multiple_of(part * SPAN, SPAN), SPAN)
        for c in range(COLS):
            total = jnp.dot(
                turned[rows, :], grads[c], preferred_element_type=jnp.float32
            ).astype(jnp.bfloat16)
            for i in range(SPAN // TILE):
                for m in range(2):
                    spot = target[m, (part * (SPAN // TILE) + i) * COLS + c]
                    tiles[spot, m] = total[i * TILE:(i + 1) * TILE, m * TILE:(m + 1) * TILE]
        lax.fori_loop(done, ready[part], send_block, 0)
        return ready[part]

    lax.fori_loop(0, WIDTH // SPAN, chunk, 0)
    for i, (out, first, count) in enumerate(outs):
        pltpu.make_async_copy(tiles.at[pl.ds(first, count)], out, sems.at[i]).wait()


def tile_work(target, ready, spots, low, gathered, grads):
    smem = pl.BlockSpec(memory_space=pltpu.SMEM)
    vmem = pl.BlockSpec(memory_space=pltpu.VMEM)
    hbm = pl.BlockSpec(memory_space=pl.ANY)
    bf16 = jnp.bfloat16
    return pl.pallas_call(
        tile_kernel,
        out_shape=tuple(
            jax.ShapeDtypeStruct((n, 2, TILE, TILE), bf16) for n in (EARLY, HALF - EARLY, HALF)
        ),
        in_specs=[smem] * 4 + [hbm, vmem],
        out_specs=(hbm,) * 3,
        scratch_shapes=[
            pltpu.VMEM((GROUP, WIDTH), bf16),
            pltpu.VMEM((WIDTH, GROUP), bf16),
            pltpu.VMEM((CAP + 1, 2, TILE, TILE), bf16),
            pltpu.SemaphoreType.DMA((ZS * YL,)),
            pltpu.SemaphoreType.DMA((3,)),
        ],
        compiler_params=pltpu.CompilerParams(vmem_limit_bytes=VMEM_LIMIT),
        cost_estimate=pl.CostEstimate(
            flops=2 * GROUP * WIDTH * 2 * HIDE, bytes_accessed=12 << 20, transcendentals=0
        ),
        name="tile_sums",
    )(target, ready, spots, low, gathered, grads)


def tables(keep_local, x, y, c):
    keep = keep_local.reshape(2, ROWS * COLS)
    places = jnp.arange(ROWS * COLS, dtype=jnp.int32)
    order = jnp.sum(jnp.where(places[None, :] <= places[:, None], keep[:, None, :], 0), axis=2) - 1
    dense_spot = (places % COLS) * ROWS + places // COLS
    slots = jnp.arange(CAP, dtype=jnp.int32)
    match = (order[:, None, :] == slots[None, :, None]) & (keep[:, None, :] == 1)
    place = DEAD + jnp.sum(jnp.where(match, dense_spot - DEAD, 0), axis=2)

    def spot_of(owner):
        dx = ((owner >> 2) - x) & (XS - 1)
        dy = ((owner >> 1) & 1) ^ y
        dc = (owner & 1) ^ c
        block = jnp.zeros_like(owner)
        for (a, b), at in BLOCKS.items():
            block = jnp.where((dx == a) & (dy == b), at, block)
        return ((1 - dc) * len(BLOCKS) + block) * PER

    target = jnp.where(keep == 1, spot_of(order >> 3) + (order & (PER - 1)), CAP)
    spots = spot_of(jnp.arange(XS * YS * CS, dtype=jnp.int32))
    chunks = jnp.arange(1, WIDTH // SPAN + 1, dtype=jnp.int32)
    inside = places[None, :] < (chunks * (SPAN // TILE * COLS))[:, None]
    counts = jnp.sum(jnp.where(inside[None], keep[:, None, :], 0), axis=2)
    ready = jnp.where(chunks == WIDTH // SPAN, XS * YS * CS, jnp.min(counts, axis=0) >> 3)
    return place.astype(jnp.int32), target.astype(jnp.int32), ready.astype(jnp.int32), spots


def piece_ranks(x, y, c):
    spots = [(0, 0), (3, 0), (1, 0), (0, 1), (2, 0), (3, 1), (1, 1), (2, 1)]
    dx = jnp.array([a for a, b in spots] * 2, jnp.int32)
    dy = jnp.array([b for a, b in spots] * 2, jnp.int32)
    dc = jnp.array([0] * len(spots) + [1] * len(spots), jnp.int32)
    return (((x + dx) & (XS - 1)) * YS + (y ^ dy)) * CS + (c ^ dc)


def body(tokens, weight_tiles, keep_mask, cotangent):
    f32, bf16 = jnp.float32, jnp.bfloat16
    rank = lax.axis_index("dp")
    x, y, c = rank >> 2, (rank >> 1) & 1, rank & 1
    low = lax.axis_index("tensor") >> 3

    other = lax.ppermute(tokens, "tensor", L_SWAP)
    own = weight_tiles[0]
    below = lax.ppermute(own, "dp", X_UP)
    above = lax.ppermute(own, "dp", X_DOWN)
    across = lax.ppermute(own, "dp", Y_SWAP)
    pair = jnp.stack([tokens, other])
    gathered = lax.all_gather(pair, "tensor", axis=0, axis_index_groups=Z_RINGS)
    place, target, ready, spots = lax.optimization_barrier(tables(keep_mask, x, y, c))
    ranks = piece_ranks(x, y, c)
    half = PER // 2
    far_low = lax.ppermute(below[:half], "dp", X_UP)
    far_high = lax.ppermute(above[half:], "dp", X_DOWN)
    far = jnp.concatenate([far_low, far_high])
    below_across = lax.ppermute(across, "dp", X_UP)
    above_across = lax.ppermute(across, "dp", X_DOWN)
    far_across = lax.ppermute(far, "dp", Y_SWAP)
    pieces = [own, below, above, across, far, below_across, above_across, far_across]
    pieces = pieces + [lax.ppermute(piece, "dp", C_SWAP) for piece in pieces]
    low_table = low.reshape(1).astype(jnp.int32)

    hidden, grads, rows = dense_work(place, ranks, low_table, pieces, gathered, cotangent)
    summed = lax.psum_scatter(rows, "tensor", scatter_dimension=0, axis_index_groups=Z_RINGS)
    early, late, keep = tile_work(target, ready, spots, low_table, gathered, grads)

    early_in = lax.ppermute(early, "dp", C_SWAP)

    def block(dx, dy, late_in=None):
        at = BLOCKS[dx, dy] * PER
        came = early_in[at:at + PER] if at < EARLY else late_in[at - EARLY:at - EARLY + PER]
        return keep[at:at + PER].astype(f32) + came.astype(f32)

    sends = [block(*at).astype(bf16) for at in ((2, 1), (1, 1), (3, 1))]
    *sends, late = lax.optimization_barrier((*sends, late))
    far_in = lax.ppermute(sends[0], "dp", Y_SWAP)
    up_in = lax.ppermute(sends[1], "dp", X_UP)
    down_in = lax.ppermute(sends[2], "dp", X_DOWN)
    late_in = lax.ppermute(late, "dp", C_SWAP)
    far_in, up_in, down_in, late_one = lax.optimization_barrier((far_in, up_in, down_in, late_in))
    far_sum = block(2, 0, late_one) + far_in.astype(f32)
    across_sum = block(0, 1, late_one) + up_in.astype(f32) + down_in.astype(f32)
    sends = lax.optimization_barrier(
        (across_sum.astype(bf16), far_sum[:half].astype(bf16), far_sum[half:].astype(bf16))
    )
    across_in = lax.ppermute(sends[0], "dp", Y_SWAP)
    half_up = lax.ppermute(sends[1], "dp", X_UP)
    half_down = lax.ppermute(sends[2], "dp", X_DOWN)
    half_up, half_down, late_two = lax.optimization_barrier((half_up, half_down, late_one))
    none = jnp.zeros_like(half_up)
    up_sum = block(1, 0, late_two) + jnp.concatenate([half_up, none]).astype(f32)
    down_sum = block(3, 0, late_two) + jnp.concatenate([none, half_down]).astype(f32)
    sends = lax.optimization_barrier((up_sum.astype(bf16), down_sum.astype(bf16)))
    up_last = lax.ppermute(sends[0], "dp", X_UP)
    down_last = lax.ppermute(sends[1], "dp", X_DOWN)
    up_last, down_last, across_in, late_three = lax.optimization_barrier(
        (up_last, down_last, across_in, late_two)
    )
    total = block(0, 0, late_three) + across_in.astype(f32)
    total = total + up_last.astype(f32) + down_last.astype(f32)
    tile_grads = (total * (1.0 / (XS * YS * CS)))[None]

    mine = jnp.where(low == 0, summed[0], summed[1])
    theirs = jnp.where(low == 0, summed[1], summed[0])
    back = lax.ppermute(theirs.astype(bf16), "tensor", L_SWAP)
    grad_tokens = (mine + back.astype(f32)).astype(bf16)
    return hidden, grad_tokens, tile_grads


def solution(mesh):
    in_specs = (
        P(("dp", "tensor"), None),
        P("tensor", "dp", None, None, None),
        P(None, None, "tensor"),
        P("dp", "tensor"),
    )
    out_specs = (P("dp", "tensor"), P(("dp", "tensor"), None), P("tensor", "dp", None, None, None))
    return jax.shard_map(body, mesh=mesh, in_specs=in_specs, out_specs=out_specs, check_vma=False)
```

```python
import jax
import jax.numpy as jnp
from jax import lax
from jax.experimental import pallas as pl
from jax.experimental.pallas import tpu as pltpu
from jax.sharding import PartitionSpec as P

TILE = 128
ROWS = 32
COLS = 7
CAP = 128
PER = 8
GROUP = 256
WIDTH = ROWS * TILE
HIDE = COLS * TILE
DEAD = ROWS * COLS
XS, YS, CS = 4, 2, 2
ZS, YL = 8, 2


def dp_perm(move):
    def index(x, y, c):
        return (x * YS + y) * CS + c

    return [
        (index(x, y, c), index(*move(x, y, c)))
        for x in range(XS)
        for y in range(YS)
        for c in range(CS)
    ]


X_UP = dp_perm(lambda x, y, c: ((x + 1) % XS, y, c))
X_DOWN = dp_perm(lambda x, y, c: ((x - 1) % XS, y, c))
Y_SWAP = dp_perm(lambda x, y, c: (x, 1 - y, c))
C_SWAP = dp_perm(lambda x, y, c: (x, y, 1 - c))
L_SWAP = [(l * ZS + z, (1 - l) * ZS + z) for l in range(YL) for z in range(ZS)]
Z_RINGS = [[l * ZS + z for z in range(ZS)] for l in range(YL)]

BLOCKS = {(1, 1): 0, (3, 1): 1, (2, 1): 2, (0, 1): 3, (2, 0): 4, (1, 0): 5, (3, 0): 6, (0, 0): 7}
EARLY = 3 * PER
HALF = len(BLOCKS) * PER
PIECES = 2 * len(BLOCKS)
SPAN = 512
VMEM_LIMIT = 58 * 1024 * 1024


def start_rows(low, gathered, tokens, sems):
    copies = []
    for z in range(ZS):
        for l in range(YL):
            first = pl.multiple_of((low[0] ^ l) * (GROUP // YL) + z * 16, 16)
            copies.append(
                pltpu.make_async_copy(
                    gathered.at[z, l], tokens.at[pl.ds(first, 16)], sems.at[z * YL + l]
                )
            )
            copies[-1].start()
    return copies


def dense_kernel(*refs):
    place, ranks, low = refs[:3]
    pieces = refs[3:3 + PIECES]
    gathered, cotangent, hidden, grads, rows_out = refs[3 + PIECES:8 + PIECES]
    weight, stored, tokens, rows, piece_sems, row_sems, out_sems = refs[8 + PIECES:]
    copies = []
    for p in range(PIECES):
        copies.append(
            pltpu.make_async_copy(pieces[p], stored.at[pl.ds(p * PER, PER)], piece_sems.at[p])
        )
        copies[-1].start()
    row_copies = start_rows(low, gathered, tokens, row_sems)
    weight[...] = jnp.zeros_like(weight)
    for p in range(PIECES):
        copies[p].wait()
        for j in range(PER):
            for m in range(2):
                spot = place[m, ranks[p] * PER + j]
                weight[spot, :, m * TILE:(m + 1) * TILE] = stored[p * PER + j, m]
    for copy in row_copies:
        copy.wait()

    for c in range(COLS):
        dense = weight[c * ROWS:(c + 1) * ROWS].reshape(WIDTH, 2 * TILE)
        total = jnp.dot(tokens[...], dense, preferred_element_type=jnp.float32)
        gate, up = total[:, :TILE], total[:, TILE:]
        lanes = slice(c * TILE, (c + 1) * TILE)
        sigma = 1.0 / (1.0 + jnp.exp(-gate))
        swish = gate * sigma
        hidden[:, lanes] = (swish * up).astype(jnp.bfloat16)
        out_grad = cotangent[:, lanes].astype(jnp.float32)
        grads[c, :, TILE:] = (out_grad * swish).astype(jnp.bfloat16)
        grads[c, :, :TILE] = (
            out_grad * up * sigma * (1.0 + gate * (1.0 - sigma))
        ).astype(jnp.bfloat16)

    span = 256
    out_copies = []
    for part in range(WIDTH // span):
        total = jnp.zeros((GROUP, span), jnp.float32)
        for c in range(COLS):
            dense = weight[c * ROWS + part * 2:c * ROWS + part * 2 + 2].reshape(span, 2 * TILE)
            total += lax.dot_general(
                grads[c], dense, (((1,), (1,)), ((), ())), preferred_element_type=jnp.float32
            )
        lanes = slice(part * span, (part + 1) * span)
        for z in range(ZS):
            for l in range(YL):
                rows[z, l, :, lanes] = total[l * 128 + z * 16:l * 128 + z * 16 + 16]
        if part % 4 == 3:
            wide = pl.ds((part - 3) * span, 4 * span)
            out_copies.append(
                pltpu.make_async_copy(
                    rows.at[:, :, :, wide], rows_out.at[:, :, :, wide], out_sems.at[part // 4]
                )
            )
            out_copies[-1].start()
    for copy in out_copies:
        copy.wait()


def dense_work(place, ranks, low, pieces, gathered, cotangent):
    smem = pl.BlockSpec(memory_space=pltpu.SMEM)
    vmem = pl.BlockSpec(memory_space=pltpu.VMEM)
    hbm = pl.BlockSpec(memory_space=pl.ANY)
    bf16 = jnp.bfloat16
    return pl.pallas_call(
        dense_kernel,
        out_shape=(
            jax.ShapeDtypeStruct((GROUP, HIDE), bf16),
            jax.ShapeDtypeStruct((COLS, GROUP, 2 * TILE), bf16),
            jax.ShapeDtypeStruct((ZS, YL, 16, WIDTH), jnp.float32),
        ),
        in_specs=[smem] * 3 + [hbm] * (PIECES + 1) + [vmem],
        out_specs=(vmem, vmem, hbm),
        scratch_shapes=[
            pltpu.VMEM((DEAD + 1, TILE, 2 * TILE), bf16),
            pltpu.VMEM((CAP, 2, TILE, TILE), bf16),
            pltpu.VMEM((GROUP, WIDTH), bf16),
            pltpu.VMEM((ZS, YL, 16, WIDTH), jnp.float32),
            pltpu.SemaphoreType.DMA((PIECES,)),
            pltpu.SemaphoreType.DMA((ZS * YL,)),
            pltpu.SemaphoreType.DMA((4,)),
        ],
        compiler_params=pltpu.CompilerParams(vmem_limit_bytes=VMEM_LIMIT),
        cost_estimate=pl.CostEstimate(
            flops=4 * GROUP * WIDTH * 2 * HIDE, bytes_accessed=16 << 20, transcendentals=GROUP * HIDE
        ),
        name="forward_and_rows",
    )(place, ranks, low, *pieces, gathered, cotangent)


def tile_kernel(
    target, ready, spots, low, gathered, grads, early_out, late_out, keep_out,
    tokens, turned, tiles, row_sems, sems,
):
    row_copies = start_rows(low, gathered, tokens, row_sems)
    tiles[...] = jnp.zeros_like(tiles)
    for copy in row_copies:
        copy.wait()
    for r in range(0, WIDTH, 512):
        turned[r:r + 512, :] = tokens[:, r:r + 512].T
    outs = [(early_out, 0, EARLY), (late_out, EARLY, HALF - EARLY), (keep_out, HALF, HALF)]

    def send_block(k, unused):
        spot = pl.multiple_of(spots[k], PER)
        for i, (out, first, count) in enumerate(outs):
            @pl.when((spot >= first) & (spot < first + count))
            def _():
                pltpu.make_async_copy(
                    tiles.at[pl.ds(spot, PER)], out.at[pl.ds(spot - first, PER)], sems.at[i]
                ).start()
        return unused

    def chunk(part, done):
        rows = pl.ds(pl.multiple_of(part * SPAN, SPAN), SPAN)
        for c in range(COLS):
            total = jnp.dot(
                turned[rows, :], grads[c], preferred_element_type=jnp.float32
            ).astype(jnp.bfloat16)
            for i in range(SPAN // TILE):
                for m in range(2):
                    spot = target[m, (part * (SPAN // TILE) + i) * COLS + c]
                    tiles[spot, m] = total[i * TILE:(i + 1) * TILE, m * TILE:(m + 1) * TILE]
        lax.fori_loop(done, ready[part], send_block, 0)
        return ready[part]

    lax.fori_loop(0, WIDTH // SPAN, chunk, 0)
    for i, (out, first, count) in enumerate(outs):
        pltpu.make_async_copy(tiles.at[pl.ds(first, count)], out, sems.at[i]).wait()


def tile_work(target, ready, spots, low, gathered, grads):
    smem = pl.BlockSpec(memory_space=pltpu.SMEM)
    vmem = pl.BlockSpec(memory_space=pltpu.VMEM)
    hbm = pl.BlockSpec(memory_space=pl.ANY)
    bf16 = jnp.bfloat16
    return pl.pallas_call(
        tile_kernel,
        out_shape=tuple(
            jax.ShapeDtypeStruct((n, 2, TILE, TILE), bf16) for n in (EARLY, HALF - EARLY, HALF)
        ),
        in_specs=[smem] * 4 + [hbm, vmem],
        out_specs=(hbm,) * 3,
        scratch_shapes=[
            pltpu.VMEM((GROUP, WIDTH), bf16),
            pltpu.VMEM((WIDTH, GROUP), bf16),
            pltpu.VMEM((CAP + 1, 2, TILE, TILE), bf16),
            pltpu.SemaphoreType.DMA((ZS * YL,)),
            pltpu.SemaphoreType.DMA((3,)),
        ],
        compiler_params=pltpu.CompilerParams(vmem_limit_bytes=VMEM_LIMIT),
        cost_estimate=pl.CostEstimate(
            flops=2 * GROUP * WIDTH * 2 * HIDE, bytes_accessed=12 << 20, transcendentals=0
        ),
        name="tile_sums",
    )(target, ready, spots, low, gathered, grads)


def tables(keep_local, x, y, c):
    keep = keep_local.reshape(2, ROWS * COLS)
    places = jnp.arange(ROWS * COLS, dtype=jnp.int32)
    order = jnp.sum(jnp.where(places[None, :] <= places[:, None], keep[:, None, :], 0), axis=2) - 1
    dense_spot = (places % COLS) * ROWS + places // COLS
    slots = jnp.arange(CAP, dtype=jnp.int32)
    match = (order[:, None, :] == slots[None, :, None]) & (keep[:, None, :] == 1)
    place = DEAD + jnp.sum(jnp.where(match, dense_spot - DEAD, 0), axis=2)

    def spot_of(owner):
        dx = ((owner >> 2) - x) & (XS - 1)
        dy = ((owner >> 1) & 1) ^ y
        dc = (owner & 1) ^ c
        block = jnp.zeros_like(owner)
        for (a, b), at in BLOCKS.items():
            block = jnp.where((dx == a) & (dy == b), at, block)
        return ((1 - dc) * len(BLOCKS) + block) * PER

    target = jnp.where(keep == 1, spot_of(order >> 3) + (order & (PER - 1)), CAP)
    spots = spot_of(jnp.arange(XS * YS * CS, dtype=jnp.int32))
    chunks = jnp.arange(1, WIDTH // SPAN + 1, dtype=jnp.int32)
    inside = places[None, :] < (chunks * (SPAN // TILE * COLS))[:, None]
    counts = jnp.sum(jnp.where(inside[None], keep[:, None, :], 0), axis=2)
    ready = jnp.where(chunks == WIDTH // SPAN, XS * YS * CS, jnp.min(counts, axis=0) >> 3)
    return place.astype(jnp.int32), target.astype(jnp.int32), ready.astype(jnp.int32), spots


def piece_ranks(x, y, c):
    spots = [(0, 0), (3, 0), (1, 0), (0, 1), (2, 0), (3, 1), (1, 1), (2, 1)]
    dx = jnp.array([a for a, b in spots] * 2, jnp.int32)
    dy = jnp.array([b for a, b in spots] * 2, jnp.int32)
    dc = jnp.array([0] * len(spots) + [1] * len(spots), jnp.int32)
    return (((x + dx) & (XS - 1)) * YS + (y ^ dy)) * CS + (c ^ dc)


def body(tokens, weight_tiles, keep_mask, cotangent):
    f32, bf16 = jnp.float32, jnp.bfloat16
    rank = lax.axis_index("dp")
    x, y, c = rank >> 2, (rank >> 1) & 1, rank & 1
    low = lax.axis_index("tensor") >> 3

    other = lax.ppermute(tokens, "tensor", L_SWAP)
    own = weight_tiles[0]
    below = lax.ppermute(own, "dp", X_UP)
    above = lax.ppermute(own, "dp", X_DOWN)
    across = lax.ppermute(own, "dp", Y_SWAP)
    pair = jnp.stack([tokens, other])
    gathered = lax.all_gather(pair, "tensor", axis=0, axis_index_groups=Z_RINGS)
    place, target, ready, spots = lax.optimization_barrier(tables(keep_mask, x, y, c))
    ranks = piece_ranks(x, y, c)
    half = PER // 2
    far_low = lax.ppermute(below[:half], "dp", X_UP)
    far_high = lax.ppermute(above[half:], "dp", X_DOWN)
    far = jnp.concatenate([far_low, far_high])
    below_across = lax.ppermute(across, "dp", X_UP)
    above_across = lax.ppermute(across, "dp", X_DOWN)
    far_across = lax.ppermute(far, "dp", Y_SWAP)
    pieces = [own, below, above, across, far, below_across, above_across, far_across]
    pieces = pieces + [lax.ppermute(piece, "dp", C_SWAP) for piece in pieces]
    low_table = low.reshape(1).astype(jnp.int32)

    hidden, grads, rows = dense_work(place, ranks, low_table, pieces, gathered, cotangent)
    summed = lax.psum_scatter(rows, "tensor", scatter_dimension=0, axis_index_groups=Z_RINGS)
    early, late, keep = tile_work(target, ready, spots, low_table, gathered, grads)

    early_in = lax.ppermute(early, "dp", C_SWAP)

    def block(dx, dy, late_in=None):
        at = BLOCKS[dx, dy] * PER
        came = early_in[at:at + PER] if at < EARLY else late_in[at - EARLY:at - EARLY + PER]
        return keep[at:at + PER].astype(f32) + came.astype(f32)

    sends = [block(*at).astype(bf16) for at in ((2, 1), (1, 1), (3, 1))]
    *sends, late = lax.optimization_barrier((*sends, late))
    far_in = lax.ppermute(sends[0], "dp", Y_SWAP)
    up_in = lax.ppermute(sends[1], "dp", X_UP)
    down_in = lax.ppermute(sends[2], "dp", X_DOWN)
    late_in = lax.ppermute(late, "dp", C_SWAP)
    far_in, up_in, down_in, late_one = lax.optimization_barrier((far_in, up_in, down_in, late_in))
    far_sum = block(2, 0, late_one) + far_in.astype(f32)
    across_sum = block(0, 1, late_one) + up_in.astype(f32) + down_in.astype(f32)
    sends = lax.optimization_barrier(
        (across_sum.astype(bf16), far_sum[:half].astype(bf16), far_sum[half:].astype(bf16))
    )
    across_in = lax.ppermute(sends[0], "dp", Y_SWAP)
    half_up = lax.ppermute(sends[1], "dp", X_UP)
    half_down = lax.ppermute(sends[2], "dp", X_DOWN)
    half_up, half_down, late_two = lax.optimization_barrier((half_up, half_down, late_one))
    none = jnp.zeros_like(half_up)
    up_sum = block(1, 0, late_two) + jnp.concatenate([half_up, none]).astype(f32)
    down_sum = block(3, 0, late_two) + jnp.concatenate([none, half_down]).astype(f32)
    sends = lax.optimization_barrier((up_sum.astype(bf16), down_sum.astype(bf16)))
    up_last = lax.ppermute(sends[0], "dp", X_UP)
    down_last = lax.ppermute(sends[1], "dp", X_DOWN)
    mine = jnp.where(low == 0, summed[0], summed[1])
    theirs = jnp.where(low == 0, summed[1], summed[0]).astype(bf16)
    back = lax.ppermute(theirs, "tensor", L_SWAP)
    up_last, down_last, across_in, late_three, theirs = lax.optimization_barrier(
        (up_last, down_last, across_in, late_two, theirs)
    )
    total = block(0, 0, late_three) + across_in.astype(f32)
    total = total + up_last.astype(f32) + down_last.astype(f32)
    tile_grads = (total * (1.0 / (XS * YS * CS)))[None]

    grad_tokens = (mine + back.astype(f32)).astype(bf16)
    return hidden, grad_tokens, tile_grads


def solution(mesh):
    in_specs = (
        P(("dp", "tensor"), None),
        P("tensor", "dp", None, None, None),
        P(None, None, "tensor"),
        P("dp", "tensor"),
    )
    out_specs = (P("dp", "tensor"), P(("dp", "tensor"), None), P("tensor", "dp", None, None, None))
    return jax.shard_map(body, mesh=mesh, in_specs=in_specs, out_specs=out_specs, check_vma=False)
```
